32 devices in a mesh: seq: 8 (over y, x, core), exp: 4 (over z).
Axes of the slice: x: 2, y: 2, z: 4, core: 2. Of those that a mesh axis runs over, the one named last changes fastest.
Arguments:
- hidden_in: float32 [24, 4, 2048], P('seq'), may hold values from -6 to 6
- cache_lens: int32 [24], replicated, may hold values from 64 to 16384, as said below
- slot_request: int32 [368], P('seq'), may hold values from -1 to 23, as said below
- slot_block: int32 [368], P('seq'), may hold values from 0 to 128, as said below
- key_cache: bfloat16 [368, 128, 2048], P('seq', None, 'exp'), may hold values from -70 to 70
- value_cache: bfloat16 [368, 128, 2048], P('seq', None, 'exp'), may hold values from -6 to 6
- attn_gain: float32 [2048], replicated, may hold values from 0.5 to 1.5
- query_weight: bfloat16 [2048, 2048], P(None, 'exp'), may hold values from -0.125 to 0.125
- key_weight: bfloat16 [2048, 2048], P(None, 'exp'), may hold values from -0.125 to 0.125
- value_weight: bfloat16 [2048, 2048], P(None, 'exp'), may hold values from -0.125 to 0.125
- out_weight: bfloat16 [2048, 2048], P('exp'), may hold values from -0.125 to 0.125
- ffn_gain: float32 [2048], replicated, may hold values from 0.5 to 1.5
- expert_ids: int32 [24, 4, 6], P('seq'), may hold values from 0 to 63, all different within a row; in each aligned block of 12 rows (0 to 11, 12 to 23, ..., all dimensions but the last counted through in order) at most 3 rows name the same one
- expert_weights: float32 [24, 4, 6], P('seq'), may hold values from 0.05 to 0.6
- gate_experts: bfloat16 [64, 2048, 1408], P('seq', None, 'exp'), may hold values from -0.125 to 0.125
- up_experts: bfloat16 [64, 2048, 1408], P('seq', None, 'exp'), may hold values from -0.125 to 0.125
- down_experts: bfloat16 [64, 1408, 2048], P('seq', 'exp'), may hold values from -0.15625 to 0.15625
- gate_shared: bfloat16 [2048, 2816], P(None, 'exp'), may hold values from -0.125 to 0.125
- up_shared: bfloat16 [2048, 2816], P(None, 'exp'), may hold values from -0.125 to 0.125
- down_shared: bfloat16 [2816, 2048], P('exp'), may hold values from -0.109375 to 0.109375
Outputs:
- hidden_out: float32 [24, 4, 2048], P('seq', None, 'exp')
- key_cache_out: bfloat16 [368, 128, 2048], P('seq', None, 'exp')
- value_cache_out: bfloat16 [368, 128, 2048], P('seq', None, 'exp')
The draws below stay inside these ranges and needn't reach their ends.
Inputs may be any that keep to these rules, and one draw needn't show every extreme that they name: `cache_lens`: exactly two requests have 16384 positions and one has 512; the others lie between 64 and 512. `slot_request`: each block of 128 positions of each request, up to position cache_lens + 3, is held by exactly one slot; -1 marks an empty slot. `slot_block`: empty slots carry 0. `expert_ids`: among the rows of one index of seq, no expert is named more than 3 times.
All inputs are finite; a program needn't handle non-finite values.
Results may differ from the reference program's by a relative error of at most 0.02.
Values may be sent and summed in bfloat16 or wider, within the bound.
No kernel may reach another device: no remote copies, remote signals or barrier semaphores. Data moves between devices by JAX's collectives and lax.ppermute only.
A program may use at most 128 MiB of HBM per device.

```python
import math
import jax
import jax.numpy as jnp
import numpy as np
from jax import lax

D = 2048
H = 16
HD = 128
EXPERTS = 64
FE = 1408
TOP = 6
SHARED_FF = 2816
STEPS = 4
BLK = 128
LONGLEN = 16384
SHORTMIN = 64
SHORTMAX = 512
REQ_DEV = 3
REQUESTS = 24
POOL = 46
CAP = 3
N_SEQ = 8


def lengths_and_slots(key):
    base = jax.random.fold_in(key, 101)
    length_key, pick_key, place_key = jax.random.split(base, 3)
    lengths = jax.random.randint(length_key, (REQUESTS,), SHORTMIN, SHORTMAX + 1, dtype=jnp.int32)
    chosen = jax.random.permutation(pick_key, REQUESTS).astype(jnp.int32)
    lengths = lengths.at[chosen[0]].set(LONGLEN).at[chosen[1]].set(LONGLEN).at[chosen[2]].set(SHORTMAX)
    block_counts = (lengths + STEPS + BLK - 1) // BLK
    ends = jnp.cumsum(block_counts).astype(jnp.int32)
    starts = ends - block_counts
    total_slots = N_SEQ * POOL
    listing = jnp.arange(total_slots, dtype=jnp.int32)
    owner = jnp.sum((starts[None, :] <= listing[:, None]).astype(jnp.int32), axis=1) - 1
    filled = listing < ends[-1]
    block_number = listing - starts[owner]
    owner = jnp.where(filled, owner, -1).astype(jnp.int32)
    block_number = jnp.where(filled, block_number, 0).astype(jnp.int32)
    placement = jax.random.permutation(place_key, total_slots).astype(jnp.int32)
    return (lengths, owner[placement], block_number[placement])


def draw_cache_lens(key, part):
    return lengths_and_slots(key)[0]


def draw_slot_request(key, part):
    return lengths_and_slots(key)[1]


def draw_slot_block(key, part):
    return lengths_and_slots(key)[2]


def draw_key_cache(key, part):
    total_slots = N_SEQ * POOL
    shape = (total_slots, BLK, H * HD)
    result = jnp.clip(jax.random.normal(key, shape, jnp.float32), -4.0, 4.0)
    return result.astype(jnp.bfloat16)


def block_levels(rng, shape, shards, low, top_value):
    def one(position, blocks):
        heights = jax.random.uniform(jax.random.fold_in(jax.random.fold_in(rng, 6), position), (blocks,), jnp.float32, low / len(shards), top_value / len(shards))
        return jnp.repeat(jnp.exp(heights), shape[position] // blocks).reshape((-1,) + (1,) * (len(shape) - position - 1))

    level = one(*shards[0])
    for cut in shards[1:]:
        level = level * one(*cut)
    return level


def routed_block(rng, own, number, rows, amount, top, reach, lean):
    order = jax.random.permutation(rng, amount)
    packed, common = portions_of(amount, rows * top, reach, lean, True), portions_of(amount, rows * top, reach, lean, False)
    places = jnp.arange(amount)

    def named(sizes, turn):
        used = int((sizes > 0).sum())
        fixed = max(1, used // 4)
        passed = fixed + (places - fixed + turn * (used - fixed)) % max(1, amount - fixed)
        return jnp.zeros((amount,), jnp.int32).at[order[jnp.where(places < fixed, places, passed)]].set(jnp.asarray(sizes, jnp.int32))

    sizes = jnp.where(number % 4 == 0, named(packed, number // 4), named(common, number - number // 4 - 1))
    mixed = jax.random.permutation(jax.random.fold_in(own, 3), amount)
    source_of, receiver = mixed[0:amount // 2 * 2:2], mixed[1:amount // 2 * 2:2]
    room = jnp.minimum(sizes[source_of] - 1, reach - sizes[receiver]) // 2
    room = jnp.where((source_of == order[0]) | (receiver == order[0]) | (sizes[receiver] == 0), 0, jnp.maximum(room, 0))
    passed = jax.random.randint(jax.random.fold_in(own, 4), (amount // 2,), 0, 1 << 20) % (room + 1)
    sizes = sizes.at[source_of].add(-passed).at[receiver].add(passed)
    items = jnp.searchsorted(jnp.cumsum(sizes), jnp.arange(rows * top), side="right").astype(jnp.int32)
    table = items.reshape(top, rows).T
    table = table[jax.random.permutation(jax.random.fold_in(own, 1), rows)]
    turn = jax.random.randint(jax.random.fold_in(own, 2), (rows, 1), 0, top)
    return jnp.take_along_axis(table, (jnp.arange(top)[None, :] + turn) % top, axis=1)


def portions_of(amount, total, bound, lean, full):
    loads = [(1 << 20) // math.isqrt(grade ** lean) + 1 for grade in range(1, amount + 1)]
    largest = bound if full else min(bound, max(-(-total // amount), total * loads[0] // sum(loads)))
    least = 1 if total - largest >= amount - 1 else 0
    given, rest = [largest] + [least] * (amount - 1), total - largest - least * (amount - 1)
    while rest > 0:
        movable = [i for i in range(1, amount) if given[i] < largest] or [i for i in range(1, amount) if given[i] < bound]
        mass, budget = sum([loads[i] for i in movable]), rest
        for i in movable:
            addition = min(bound - given[i], max(1, budget * loads[i] // mass), rest)
            given[i] = given[i] + addition
            rest = rest - addition
    return np.array(given)


def gaussian(rng, extent, deviation, bound, cuts=(), kind=jnp.bfloat16):
    loudness = block_levels(rng, extent, cuts, -0.22, 0.18) if cuts else 1.0
    drawn = jax.random.normal(rng, extent, jnp.float32) * deviation * loudness
    return jnp.minimum(jnp.maximum(drawn, -bound), bound).astype(kind)


def setup_inputs(seed: int = 0) -> dict:
    arg_keys = jax.random.split(jax.random.key(seed), 21)
    hidden_in = gaussian(arg_keys[0], (REQUESTS, STEPS, D), 1.0, 6.0, ((0, 8),), jnp.float32)
    cache_lens = draw_cache_lens(jax.random.fold_in(arg_keys[20], 71), 0)
    slot_request = draw_slot_request(jax.random.fold_in(arg_keys[20], 71), 0)
    slot_block = draw_slot_block(jax.random.fold_in(arg_keys[20], 71), 0)
    key_cache = draw_key_cache(jax.random.fold_in(arg_keys[20], 71), 0)
    value_cache = gaussian(arg_keys[5], (N_SEQ * POOL, BLK, H * HD), 1.0, 6.0, ((0, 8), (2, 4)))
    attn_gain = jnp.clip(1.0 + 0.1 * jax.random.normal(arg_keys[6], (D,), jnp.float32), 0.5, 1.5)
    query_weight = gaussian(arg_keys[7], (D, H * HD), D ** -0.5, 0.125, ((1, 4),))
    key_weight = gaussian(arg_keys[8], (D, H * HD), D ** -0.5, 0.125, ((1, 4),))
    value_weight = gaussian(arg_keys[9], (D, H * HD), D ** -0.5, 0.125, ((1, 4),))
    out_weight = gaussian(arg_keys[10], (H * HD, D), (H * HD) ** -0.5, 0.125, ((0, 4),))
    ffn_gain = jnp.clip(1.0 + 0.1 * jax.random.normal(arg_keys[11], (D,), jnp.float32), 0.5, 1.5)
    expert_ids_keys = jax.random.split(jax.random.fold_in(arg_keys[12], 1), REQUESTS * STEPS // (REQ_DEV * STEPS))
    expert_ids_turns = jax.random.permutation(jax.random.fold_in(arg_keys[12], 3), REQUESTS * STEPS // (REQ_DEV * STEPS))
    expert_ids = jax.vmap(lambda own, number: routed_block(jax.random.fold_in(arg_keys[12], 2), own, number, REQ_DEV * STEPS, EXPERTS, TOP, CAP, 2))(expert_ids_keys, expert_ids_turns).reshape((REQUESTS, STEPS, TOP))
    expert_weights = jnp.clip(0.05 + 0.55 * jax.random.uniform(arg_keys[13], (REQUESTS, STEPS, TOP), jnp.float32) ** block_levels(arg_keys[13], (REQUESTS, STEPS, TOP), ((0, 8),), -0.2, 0.2), 0.05, 0.6)
    gate_experts = gaussian(arg_keys[14], (EXPERTS, D, FE), D ** -0.5, 0.125, ((0, 8), (2, 4)))
    up_experts = gaussian(arg_keys[15], (EXPERTS, D, FE), D ** -0.5, 0.125, ((0, 8), (2, 4)))
    down_experts = gaussian(arg_keys[16], (EXPERTS, FE, D), FE ** -0.5, 0.15625, ((0, 8), (1, 4)))
    gate_shared = gaussian(arg_keys[17], (D, SHARED_FF), D ** -0.5, 0.125, ((1, 4),))
    up_shared = gaussian(arg_keys[18], (D, SHARED_FF), D ** -0.5, 0.125, ((1, 4),))
    down_shared = gaussian(arg_keys[19], (SHARED_FF, D), SHARED_FF ** -0.5, 0.109375, ((0, 4),))
    return dict(hidden_in=hidden_in, cache_lens=cache_lens, slot_request=slot_request, slot_block=slot_block, key_cache=key_cache, value_cache=value_cache, attn_gain=attn_gain, query_weight=query_weight, key_weight=key_weight, value_weight=value_weight, out_weight=out_weight, ffn_gain=ffn_gain, expert_ids=expert_ids, expert_weights=expert_weights, gate_experts=gate_experts, up_experts=up_experts, down_experts=down_experts, gate_shared=gate_shared, up_shared=up_shared, down_shared=down_shared)


def rms_scale(values, gain):
    mean_square = lax.optimization_barrier(jnp.mean(values * values, axis=-1, keepdims=True))
    return values * lax.rsqrt(mean_square + 1e-06) * gain

def rotate(vectors, positions):
    half_size = vectors.shape[-1] // 2
    exponent = jnp.arange(half_size, dtype=jnp.float32) * (2.0 / vectors.shape[-1])
    frequency = jnp.power(jnp.float32(10000.0), -exponent)
    angles = positions.astype(jnp.float32)[..., None] * frequency
    cosine = jnp.cos(angles)[..., None, :]
    sine = jnp.sin(angles)[..., None, :]
    first_half = vectors[..., :half_size]
    second_half = vectors[..., half_size:]
    return jnp.concatenate([first_half * cosine - second_half * sine, second_half * cosine + first_half * sine], axis=-1)

def append_rows(cache, new_rows, slot_valid, slot_req, rel_pos):
    updated = cache
    for step_index in range(new_rows.shape[1]):
        hit_mask = slot_valid[:, None] & (rel_pos == step_index)
        updated = jnp.where(hit_mask[..., None], new_rows[slot_req, step_index][:, None, :], updated)
    return updated

def slot_partials(queries, keys, values, slot_valid, slot_req, slot_block, lengths):
    pool_count, block_size, full_width = keys.shape
    steps, heads, head_size = (queries.shape[1], queries.shape[2], queries.shape[3])
    slot_queries = queries[slot_req]
    key_heads = keys.reshape(pool_count, block_size, heads, head_size)
    value_heads = values.reshape(pool_count, block_size, heads, head_size)
    scores = jnp.einsum('pthd,pkhd->pthk', slot_queries.astype(jnp.float32), key_heads.astype(jnp.float32)) / math.sqrt(head_size)
    positions = slot_block[:, None] * block_size + jnp.arange(block_size, dtype=jnp.int32)[None, :]
    limits = lengths[slot_req][:, None] + jnp.arange(steps, dtype=jnp.int32)[None, :] + 1
    allowed = slot_valid[:, None, None] & (positions[:, None, :] < limits[:, :, None])
    allowed = allowed[:, :, None, :]
    block_max = lax.optimization_barrier(jnp.max(jnp.where(allowed, scores, -1e+30), axis=-1))
    safe_max = jnp.where(block_max > -1e+29, block_max, 0.0)
    weights = jnp.where(allowed, jnp.exp(scores - safe_max[..., None]), 0.0)
    totals = lax.optimization_barrier(jnp.sum(weights, axis=-1))
    rounded = weights.astype(jnp.bfloat16)
    outputs = jnp.einsum('pthk,pkhd->pthd', rounded.astype(jnp.float32), value_heads.astype(jnp.float32))
    return (block_max, totals, outputs)

def request_partials(block_max, totals, outputs, slot_valid, slot_req, requests):
    owner = slot_valid[:, None] & (slot_req[:, None] == jnp.arange(requests, dtype=jnp.int32)[None, :])
    request_max = lax.optimization_barrier(jnp.max(jnp.where(owner[:, :, None, None], block_max[:, None], -1e+30), axis=0))
    factor = jnp.where(slot_valid[:, None, None], jnp.exp(block_max - request_max[slot_req]), 0.0)
    owner_float = owner.astype(jnp.float32)
    request_total = jnp.einsum('pb,pth->bth', owner_float, totals * factor, precision=lax.Precision.HIGHEST)
    request_output = jnp.einsum('pb,pthd->bthd', owner_float, outputs * factor[..., None], precision=lax.Precision.HIGHEST)
    return (request_max, request_total, request_output)

def reference(hidden_in, cache_lens, slot_request, slot_block, key_cache, value_cache, attn_gain, query_weight, key_weight, value_weight, out_weight, ffn_gain, expert_ids, expert_weights, gate_experts, up_experts, down_experts, gate_shared, up_shared, down_shared):
    requests, steps, width = hidden_in.shape
    flat = hidden_in.reshape(requests * steps, width)
    normed = rms_scale(flat, attn_gain).astype(jnp.bfloat16)
    positions = cache_lens[:, None] + jnp.arange(steps, dtype=jnp.int32)[None, :]
    query_full = jnp.dot(normed, query_weight, preferred_element_type=jnp.float32).reshape(requests, steps, H, HD)
    queries = rotate(query_full, positions).astype(jnp.bfloat16)
    key_full = jnp.dot(normed, key_weight, preferred_element_type=jnp.float32).reshape(requests, steps, H, HD)
    new_keys = rotate(key_full, positions).astype(jnp.bfloat16).reshape(requests, steps, H * HD)
    new_values = jnp.dot(normed, value_weight, preferred_element_type=jnp.float32).astype(jnp.bfloat16).reshape(requests, steps, H * HD)
    slot_valid = slot_request >= 0
    slot_req = jnp.where(slot_valid, slot_request, 0).astype(jnp.int32)
    rel_pos = slot_block[:, None] * BLK + jnp.arange(BLK, dtype=jnp.int32)[None, :] - cache_lens[slot_req][:, None]
    key_out = append_rows(key_cache, new_keys, slot_valid, slot_req, rel_pos)
    value_out = append_rows(value_cache, new_values, slot_valid, slot_req, rel_pos)
    block_max, totals, outputs = slot_partials(queries, key_out, value_out, slot_valid, slot_req, slot_block, cache_lens)
    request_max, request_total, request_output = request_partials(block_max, totals, outputs, slot_valid, slot_req, requests)
    attended = (request_output / request_total[..., None]).astype(jnp.bfloat16).reshape(requests * steps, H * HD)
    residual = flat + jnp.dot(attended, out_weight, preferred_element_type=jnp.float32)
    ffn_in = rms_scale(residual, ffn_gain).astype(jnp.bfloat16)
    shared_inner = (jax.nn.silu(jnp.dot(ffn_in, gate_shared, preferred_element_type=jnp.float32)) * jnp.dot(ffn_in, up_shared, preferred_element_type=jnp.float32)).astype(jnp.bfloat16)
    shared_out = jnp.dot(shared_inner, down_shared, preferred_element_type=jnp.float32)
    flat_ids = expert_ids.reshape(requests * steps, TOP)
    flat_gates = expert_weights.reshape(requests * steps, TOP)
    coefficient = lax.optimization_barrier(jnp.sum(jnp.where(flat_ids[:, :, None] == jnp.arange(EXPERTS, dtype=jnp.int32)[None, None, :], flat_gates[:, :, None], 0.0), axis=1))

    def expert_step(total, inputs):
        gate_matrix, up_matrix, down_matrix, column = inputs
        inner = (jax.nn.silu(jnp.dot(ffn_in, gate_matrix, preferred_element_type=jnp.float32)) * jnp.dot(ffn_in, up_matrix, preferred_element_type=jnp.float32)).astype(jnp.bfloat16)
        return (total + column[:, None] * jnp.dot(inner, down_matrix, preferred_element_type=jnp.float32), None)
    start_total = jnp.zeros((requests * steps, width), jnp.float32)
    scanned = lax.scan(expert_step, start_total, (gate_experts, up_experts, down_experts, coefficient.T))
    result = residual + scanned[0] + shared_out
    return (result.reshape(requests, steps, width), key_out, value_out)
```

```python
import functools
import math

import jax
import jax.numpy as jnp
import numpy as np
from jax import lax
from jax.experimental import pallas as pl
from jax.experimental.pallas import tpu as pltpu
from jax.sharding import PartitionSpec as P

HD = 128
EXPERTS = 64
GROUP = 16
CHUNK = 8
NEG = -1e30
MIB = 1 << 20
F32 = jnp.float32
BF16 = jnp.bfloat16


def vmem():
    return pl.BlockSpec(memory_space=pltpu.VMEM)


def smem():
    return pl.BlockSpec(memory_space=pltpu.SMEM)


def hbm():
    return pl.BlockSpec(memory_space=pl.ANY)


def dot_nt(a, b):
    return lax.dot_general(a, b, (((1,), (1,)), ((), ())), preferred_element_type=F32)


def dot_nn(a, b):
    return jnp.dot(a, b, preferred_element_type=F32)


def iota(shape, dim):
    return lax.broadcasted_iota(jnp.int32, shape, dim)


def norm_kernel(hidden_ref, gain_ref, out_ref, rows_ref):
    local, steps, _ = hidden_ref.shape
    rows_ref[...] = jnp.zeros_like(rows_ref)
    for j in range(local):
        rows_ref[pl.ds(j * steps, steps), :] = hidden_ref[j]
    rows = rows_ref[...]
    mean_square = jnp.mean(rows * rows, axis=-1, keepdims=True)
    out_ref[...] = (rows * lax.rsqrt(mean_square + 1e-06) * gain_ref[...]).astype(BF16)


def norm_rows(hidden, gain):
    width = hidden.shape[2]
    return pl.pallas_call(
        norm_kernel,
        out_shape=jax.ShapeDtypeStruct((GROUP, width), BF16),
        in_specs=[vmem(), vmem()],
        out_specs=vmem(),
        scratch_shapes=[pltpu.VMEM((GROUP, width), F32)],
        compiler_params=pltpu.CompilerParams(vmem_limit_bytes=4 * MIB),
        name="norm_rows",
    )(hidden, gain.reshape(1, width))


def rotated(full, cosine, sine):
    heads = full.shape[1] // HD
    parts = []
    for h in range(heads):
        one = full[:, h * HD : (h + 1) * HD]
        parts.append(one * cosine + pltpu.roll(one, HD // 2, 1) * sine)
    return jnp.concatenate(parts, axis=1)


def attention_kernel(
    local,
    steps,
    lens_ref,
    slot_req_ref,
    slot_block_ref,
    rows_ref,
    cos_ref,
    sin_ref,
    query_hbm,
    key_hbm,
    value_hbm,
    key_in,
    value_in,
    part_ref,
    key_out,
    value_out,
    weights,
    key_buf,
    value_buf,
    spread,
    new_keys,
    new_values,
    slot_max,
    slot_total,
    slot_out,
    req_max,
    req_total,
    req_out,
    weight_sem,
    in_sem,
    out_sem,
):
    pool, block, width = key_buf.shape
    heads = width // HD
    per = heads * steps
    requests = req_max.shape[0]
    groups = requests // local
    chunks = [(c, min(c + CHUNK, pool)) for c in range(0, pool, CHUNK)]

    weight_copies = [
        pltpu.make_async_copy(src, weights.at[i], weight_sem.at[i])
        for i, src in enumerate((query_hbm, key_hbm, value_hbm))
    ]
    for copy in weight_copies:
        copy.start()

    def both(sources, targets, sems, i):
        low, high = chunks[i]
        return [
            pltpu.make_async_copy(
                src.at[pl.ds(low, high - low)], dst.at[pl.ds(low, high - low)], sems.at[n, i]
            )
            for n, (src, dst) in enumerate(zip(sources, targets))
        ]

    incoming = [both((key_in, value_in), (key_buf, value_buf), in_sem, i) for i in range(len(chunks))]
    outgoing = [both((key_buf, value_buf), (key_out, value_out), out_sem, i) for i in range(len(chunks))]
    for pair in incoming:
        for copy in pair:
            copy.start()

    rows = rows_ref[...]
    cosine = cos_ref[...]
    sine = sin_ref[...]
    weight_copies[0].wait()
    queries = rotated(dot_nn(rows, weights[0]), cosine, sine).astype(BF16)
    picked = iota((requests * per, rows.shape[0]), 0)
    request, inside = picked // per, picked % per
    source = request // local * GROUP + request % local * steps + inside % steps
    choose = (source == iota(picked.shape, 1)).astype(BF16)
    wide = dot_nn(choose, queries)
    head_of = iota(wide.shape, 0) % per // steps
    spread[...] = (
        jnp.where(head_of == iota(wide.shape, 1) // HD, wide, 0.0)
        .astype(BF16)
        .reshape(requests, per, width)
    )
    weight_copies[1].wait()
    new_keys[...] = rotated(dot_nn(rows, weights[1]), cosine, sine).astype(BF16).astype(F32)
    weight_copies[2].wait()
    new_values[...] = dot_nn(rows, weights[2]).astype(BF16).astype(F32)

    row_step = iota((per, block), 0) % steps
    position = iota((per, block), 1)
    scale = 1.0 / math.sqrt(HD)
    patch_rows = iota((16, width), 0)

    def slot_facts(s):
        wanted = slot_req_ref[s]
        request = jnp.maximum(wanted, 0)
        base = lens_ref[request] - slot_block_ref[s] * block
        return request, jnp.where(wanted >= 0, base, -4 * block)

    def patch(s, carry):
        request, base = slot_facts(s)

        @pl.when((base > -steps) & (base < block))
        def _():
            first = request // local * GROUP + request % local * steps
            for t in range(steps):
                row = base + t

                @pl.when((row >= 0) & (row < block))
                def _():
                    start = pl.multiple_of(row // 16 * 16, 16)
                    hit = patch_rows == row - start
                    for buf, new in ((key_buf, new_keys), (value_buf, new_values)):
                        old = buf[s, pl.ds(start, 16), :].astype(F32)
                        fresh = new[pl.ds(first + t, 1), :]
                        buf[s, pl.ds(start, 16), :] = jnp.where(hit, fresh, old).astype(BF16)

        return carry

    for i, (low, high) in enumerate(chunks):
        for copy in incoming[i]:
            copy.wait()
        lax.fori_loop(low, high, patch, 0)
        for copy in outgoing[i]:
            copy.start()
        for s in range(low, high):
            request, base = slot_facts(s)
            scores = dot_nt(spread[request], key_buf[s]) * scale
            allowed = position - row_step <= base
            scores = jnp.where(allowed, scores, NEG)
            top = jnp.max(scores, axis=-1, keepdims=True)
            weight = jnp.where(allowed, jnp.exp(scores - top), 0.0)
            total = jnp.sum(weight, axis=-1, keepdims=True)
            mixed = dot_nn(weight.astype(BF16), value_buf[s])
            result = mixed[:, :HD]
            lane_head = iota((per, HD), 0) // steps
            for h in range(1, heads):
                result = jnp.where(lane_head == h, mixed[:, h * HD : (h + 1) * HD], result)
            slot_max[s] = jnp.broadcast_to(top, (per, HD))
            slot_total[s] = jnp.broadcast_to(total, (per, HD))
            slot_out[s] = result

    req_max[...] = jnp.full_like(req_max, NEG)
    req_total[...] = jnp.zeros_like(req_total)
    req_out[...] = jnp.zeros_like(req_out)

    def find_max(s, carry):
        request = jnp.maximum(slot_req_ref[s], 0)
        req_max[request] = jnp.maximum(req_max[request], slot_max[s])
        return carry

    lax.fori_loop(0, pool, find_max, 0)

    def add_up(s, carry):
        request = jnp.maximum(slot_req_ref[s], 0)
        factor = jnp.exp(slot_max[s] - req_max[request])
        req_total[request] = req_total[request] + factor * slot_total[s]
        req_out[request] = req_out[request] + factor * slot_out[s]
        return carry

    lax.fori_loop(0, pool, add_up, 0)

    total = req_total[...]
    some = total > 0.0
    safe = jnp.where(some, total, 1.0)
    mean = jnp.where(some, req_out[...] / safe, 0.0).astype(BF16)
    level = jnp.where(some, req_max[...] + jnp.log(safe), NEG)
    high = level.astype(BF16).astype(F32)
    middle = (level - high).astype(BF16).astype(F32)
    low_part = (level - high - middle).astype(BF16).astype(F32)
    row = iota(level.shape, 1)
    lane = iota(level.shape, 2)
    packed = jnp.where(lane == row, high, 0.0)
    packed = packed + jnp.where(lane == row + per, middle, 0.0)
    packed = packed + jnp.where(lane == row + 2 * per, low_part, 0.0)
    packed = jnp.sum(packed, axis=1, keepdims=True)
    block_row = iota((16, HD), 0)
    for g in range(groups):
        levels = jnp.zeros((16, HD), F32)
        for j in range(local):
            b = g * local + j
            part_ref[g, pl.ds(j * per, per), :] = mean[b]
            levels = jnp.where(block_row == j, packed[b], levels)
        part_ref[g, pl.ds(local * per, 16), :] = levels.astype(BF16)
    for pair in outgoing:
        for copy in pair:
            copy.wait()


def attention(rows, cosine, sine, weights, caches, lens, slot_req, slot_block, local, steps):
    pool, block, width = caches[0].shape
    model = rows.shape[1]
    requests = lens.shape[0]
    per = width // HD * steps
    chunk_count = -(-pool // CHUNK)
    cache_shape = jax.ShapeDtypeStruct(caches[0].shape, BF16)
    return pl.pallas_call(
        functools.partial(attention_kernel, local, steps),
        out_shape=(
            jax.ShapeDtypeStruct((requests // local, local * per + 16, HD), BF16),
            cache_shape,
            cache_shape,
        ),
        in_specs=[smem()] * 3 + [vmem()] * 3 + [hbm()] * 5,
        out_specs=(vmem(), hbm(), hbm()),
        scratch_shapes=[
            pltpu.VMEM((3, model, width), BF16),
            pltpu.VMEM((pool, block, width), BF16),
            pltpu.VMEM((pool, block, width), BF16),
            pltpu.VMEM((requests, per, width), BF16),
            pltpu.VMEM((rows.shape[0], width), F32),
            pltpu.VMEM((rows.shape[0], width), F32),
            pltpu.VMEM((pool, per, HD), F32),
            pltpu.VMEM((pool, per, HD), F32),
            pltpu.VMEM((pool, per, HD), F32),
            pltpu.VMEM((requests, per, HD), F32),
            pltpu.VMEM((requests, per, HD), F32),
            pltpu.VMEM((requests, per, HD), F32),
            pltpu.SemaphoreType.DMA((3,)),
            pltpu.SemaphoreType.DMA((2, chunk_count)),
            pltpu.SemaphoreType.DMA((2, chunk_count)),
        ],
        compiler_params=pltpu.CompilerParams(vmem_limit_bytes=36 * MIB),
        name="attention",
    )(lens, slot_req, slot_block, rows, cosine, sine, *weights, *caches)


def merge_kernel(local, steps, part_ref, weight_ref, out_ref):
    holders = part_ref.shape[0]
    width = weight_ref.shape[0]
    heads = width // HD
    per = heads * steps
    count = local * per
    values = [part_ref[g, pl.ds(0, count), :].astype(F32) for g in range(holders)]
    row = iota((count, HD), 0)
    lane = iota((count, HD), 1)
    mine = (lane % per == row % per) & (lane < 3 * per)
    levels = []
    for g in range(holders):
        stat = part_ref[g, pl.ds(count, 16), :].astype(F32)
        wide = jnp.concatenate(
            [jnp.broadcast_to(stat[j : j + 1], (per, HD)) for j in range(local)], axis=0
        )
        levels.append(jnp.sum(jnp.where(mine, wide, 0.0), axis=-1, keepdims=True))
    top = functools.reduce(jnp.maximum, levels)
    shares = [jnp.exp(level - top) for level in levels]
    total = sum(shares)
    mixed = sum(share * value for share, value in zip(shares, values))
    attended = (mixed / total).astype(BF16)
    target = iota((GROUP, count), 0)
    source = iota((GROUP, count), 1)
    parts = []
    for h in range(heads):
        pick = (source == target // steps * per + h * steps + target % steps) & (
            target < local * steps
        )
        parts.append(dot_nn(pick.astype(BF16), attended).astype(BF16))
    out_ref[...] = dot_nn(jnp.concatenate(parts, axis=1), weight_ref[...]).astype(BF16)


def merge_project(parts, out_weight, local, steps):
    return pl.pallas_call(
        functools.partial(merge_kernel, local, steps),
        out_shape=jax.ShapeDtypeStruct((GROUP, out_weight.shape[1]), BF16),
        in_specs=[vmem(), vmem()],
        out_specs=vmem(),
        compiler_params=pltpu.CompilerParams(vmem_limit_bytes=8 * MIB),
        name="merge_project",
    )(parts, out_weight)


def second_norm_kernel(hidden_ref, left_ref, right_ref, gain_ref, ids_ref, gates_ref, rows_out, res_out, rows_ref):
    local, steps, width = hidden_ref.shape
    rows_ref[...] = jnp.zeros_like(rows_ref)
    for j in range(local):
        rows_ref[pl.ds(j * steps, steps), :] = hidden_ref[j]
    residual = rows_ref[...] + (left_ref[...].astype(F32) + right_ref[...].astype(F32))
    res_out[...] = residual
    mean_square = jnp.mean(residual * residual, axis=-1, keepdims=True)
    normed = residual * lax.rsqrt(mean_square + 1e-06) * gain_ref[...]
    rows_out[:, pl.ds(0, width)] = normed.astype(BF16)
    rows_ref[:, pl.ds(0, HD)] = jnp.zeros((GROUP, HD), F32)
    lane = iota((steps, HD), 1)
    for j in range(local):
        table = jnp.zeros((steps, HD), F32)
        for k in range(ids_ref.shape[2]):
            hit = lane % EXPERTS == ids_ref[j, :, k : k + 1]
            table = table + jnp.where(hit, gates_ref[j, :, k : k + 1], 0.0)
        rows_ref[pl.ds(j * steps, steps), pl.ds(0, HD)] = table
    table = rows_ref[:, pl.ds(0, HD)]
    high = table.astype(BF16)
    low = (table - high.astype(F32)).astype(BF16)
    rows_out[:, pl.ds(width, HD)] = jnp.where(iota((GROUP, HD), 1) < EXPERTS, high.astype(F32), low.astype(F32)).astype(BF16)


def second_norm(hidden, left, right, gain, ids, gates):
    width = hidden.shape[2]
    return pl.pallas_call(
        second_norm_kernel,
        out_shape=(
            jax.ShapeDtypeStruct((GROUP, width + HD), BF16),
            jax.ShapeDtypeStruct((GROUP, width), F32),
        ),
        in_specs=[vmem()] * 6,
        out_specs=(vmem(), vmem()),
        scratch_shapes=[pltpu.VMEM((GROUP, width), F32)],
        compiler_params=pltpu.CompilerParams(vmem_limit_bytes=4 * MIB),
        name="second_norm",
    )(hidden, left, right, gain.reshape(1, width), ids, gates)


def shared_kernel(rows_ref, gate_ref, up_ref, down_ref, out_ref):
    rows = rows_ref[:, pl.ds(0, down_ref.shape[1])]
    inner = jax.nn.silu(dot_nt(rows, gate_ref[...])) * dot_nt(rows, up_ref[...])
    out_ref[...] = dot_nn(inner.astype(BF16), down_ref[...])


def shared_experts(rows, gate, up, down):
    return pl.pallas_call(
        shared_kernel,
        out_shape=jax.ShapeDtypeStruct((GROUP, down.shape[1]), F32),
        in_specs=[vmem()] * 4,
        out_specs=vmem(),
        compiler_params=pltpu.CompilerParams(vmem_limit_bytes=16 * MIB),
        name="shared_experts",
    )(rows, gate, up, down)


def experts_kernel(tokens, place_ref, rows_ref, shared_ref, gate_ref, up_ref, down_ref, out_ref, total_ref):
    e = pl.program_id(0)
    count = pl.num_programs(0)
    width = down_ref.shape[2]
    seq_rank = place_ref[0]
    first = place_ref[1]

    @pl.when(e == 0)
    def _():
        total_ref[...] = jnp.zeros_like(total_ref)
        start = pl.multiple_of(seq_rank * GROUP, GROUP)
        total_ref[pl.ds(start, GROUP), :] = shared_ref[...]

    rows = rows_ref[:, pl.ds(0, width)]
    table = rows_ref[:, pl.ds(width, HD)].astype(F32)
    mine = iota(table.shape, 1) % EXPERTS == first + e
    share = jnp.sum(jnp.where(mine, table, 0.0), axis=-1, keepdims=True)
    gate = dot_nt(rows, gate_ref[0])
    up = dot_nt(rows, up_ref[0])
    inner = (jax.nn.silu(gate) * up * share).astype(BF16)
    total_ref[...] += dot_nn(inner, down_ref[0])

    @pl.when(e == count - 1)
    def _():
        groups = total_ref.shape[0] // GROUP
        pieces = out_ref.shape[0] // groups
        columns = width // pieces
        for g in range(groups):
            for p in range(pieces):
                out_ref[g * pieces + p] = total_ref[
                    pl.ds(g * GROUP, tokens), pl.ds(p * columns, columns)
                ].astype(BF16)


def routed_experts(place, rows, shared, gate, up, down, tokens, pieces):
    count, hidden, width = down.shape
    groups = rows.shape[0] // GROUP
    one = pl.BlockSpec((1, hidden, width), lambda e: (e, 0, 0))
    return pl.pallas_call(
        functools.partial(experts_kernel, tokens),
        grid=(count,),
        out_shape=jax.ShapeDtypeStruct((groups * pieces, tokens, width // pieces), BF16),
        in_specs=[smem(), vmem(), vmem(), one, one, one],
        out_specs=vmem(),
        scratch_shapes=[pltpu.VMEM((rows.shape[0], width), F32)],
        compiler_params=pltpu.CompilerParams(vmem_limit_bytes=24 * MIB),
        name="routed_experts",
    )(place, rows, shared, gate, up, down)


def last_kernel(rank_ref, res_ref, parts_ref, out_ref):
    local, steps, columns = out_ref.shape
    total = parts_ref[0].astype(F32)
    for i in range(1, parts_ref.shape[0]):
        total = total + parts_ref[i].astype(F32)
    start = pl.multiple_of(rank_ref[0] * columns, HD)
    total = total + res_ref[pl.ds(0, local * steps), pl.ds(start, columns)]
    for j in range(local):
        out_ref[j] = total[j * steps : (j + 1) * steps]


def last_sum(rank, residual, parts, local, steps):
    return pl.pallas_call(
        last_kernel,
        out_shape=jax.ShapeDtypeStruct((local, steps, parts.shape[2]), F32),
        in_specs=[smem(), vmem(), vmem()],
        out_specs=vmem(),
        compiler_params=pltpu.CompilerParams(vmem_limit_bytes=8 * MIB),
        name="last_sum",
    )(rank, residual, parts)


def partner(array, axis, bit):
    count = lax.axis_size(axis)
    return lax.ppermute(array, axis, [(i, i ^ bit) for i in range(count)])


def rotation_tables(lens, local, steps):
    half = HD // 2
    frequency = np.power(10000.0, -np.arange(half, dtype=np.float64) * (2.0 / HD)).astype(np.float32)
    both = jnp.asarray(np.concatenate([frequency, frequency]))
    sign = jnp.asarray(np.concatenate([-np.ones(half), np.ones(half)]).astype(np.float32))
    positions = lens.reshape(-1, local, 1) + jnp.arange(steps, dtype=jnp.int32)
    positions = positions.reshape(-1, local * steps)
    positions = jnp.pad(positions, ((0, 0), (0, GROUP - local * steps))).reshape(-1, 1)
    angles = positions.astype(F32) * both
    return jnp.cos(angles), jnp.sin(angles) * sign


def body(
    hidden_in,
    cache_lens,
    slot_request,
    slot_block,
    key_cache,
    value_cache,
    attn_gain,
    query_weight,
    key_weight,
    value_weight,
    out_weight,
    ffn_gain,
    expert_ids,
    expert_weights,
    gate_experts,
    up_experts,
    down_experts,
    gate_shared,
    up_shared,
    down_shared,
):
    local, steps, width = hidden_in.shape
    exp_count = lax.axis_size("exp")
    seq_rank = lax.axis_index("seq").astype(jnp.int32)
    exp_rank = lax.axis_index("exp").astype(jnp.int32)
    tokens = local * steps

    cosine, sine = rotation_tables(cache_lens, local, steps)
    normed = norm_rows(hidden_in, attn_gain)
    rows = lax.all_gather(normed, "seq", axis=0, tiled=True)
    parts, key_out, value_out = attention(
        rows,
        cosine,
        sine,
        (query_weight, key_weight, value_weight),
        (key_cache, value_cache),
        cache_lens,
        slot_request,
        slot_block,
        local,
        steps,
    )
    parts = lax.all_to_all(parts, "seq", split_axis=0, concat_axis=0, tiled=True)
    terms = merge_project(parts, out_weight, local, steps)
    other = partner(terms, "exp", 1)
    bit = 2
    while bit < exp_count:
        terms = (terms.astype(F32) + other.astype(F32)).astype(BF16)
        other = partner(terms, "exp", bit)
        bit *= 2
    ffn_in, residual = second_norm(
        hidden_in, terms, other, ffn_gain, expert_ids, expert_weights
    )
    shared = shared_experts(
        ffn_in, jnp.swapaxes(gate_shared, 0, 1), jnp.swapaxes(up_shared, 0, 1), down_shared
    )
    all_rows = lax.all_gather(ffn_in, "seq", axis=0, tiled=True)
    place = jnp.stack([seq_rank, seq_rank * gate_experts.shape[0]])
    sums = routed_experts(
        place,
        all_rows,
        shared,
        jnp.swapaxes(gate_experts, 1, 2),
        jnp.swapaxes(up_experts, 1, 2),
        down_experts,
        tokens,
        exp_count,
    )
    sums = lax.all_to_all(sums, ("seq", "exp"), split_axis=0, concat_axis=0, tiled=True)
    hidden_out = last_sum(exp_rank.reshape(1), residual, sums, local, steps)
    return hidden_out, key_out, value_out


def solution(mesh):
    in_specs = (
        P("seq", None, None),
        P(),
        P("seq"),
        P("seq"),
        P("seq", None, "exp"),
        P("seq", None, "exp"),
        P(),
        P(None, "exp"),
        P(None, "exp"),
        P(None, "exp"),
        P("exp", None),
        P(),
        P("seq", None, None),
        P("seq", None, None),
        P("seq", None, "exp"),
        P("seq", None, "exp"),
        P("seq", "exp", None),
        P(None, "exp"),
        P(None, "exp"),
        P("exp", None),
    )
    out_specs = (P("seq", None, "exp"), P("seq", None, "exp"), P("seq", None, "exp"))
    return jax.shard_map(body, mesh=mesh, in_specs=in_specs, out_specs=out_specs, check_vma=False)
```

```python
import functools
import math

import jax
import jax.numpy as jnp
import numpy as np
from jax import lax
from jax.experimental import pallas as pl
from jax.experimental.pallas import tpu as pltpu
from jax.sharding import PartitionSpec as P

HD = 128
EXPERTS = 64
GROUP = 16
BLOCK = 768
AHEAD = 3
CHUNK = 16
NEG = -1e30
MIB = 1 << 20
F32 = jnp.float32
BF16 = jnp.bfloat16


def vmem():
    return pl.BlockSpec(memory_space=pltpu.VMEM)


def smem():
    return pl.BlockSpec(memory_space=pltpu.SMEM)


def hbm():
    return pl.BlockSpec(memory_space=pl.ANY)


def far(array):
    return pltpu.with_memory_space_constraint(array, pltpu.HBM)


def dot_nt(a, b):
    return lax.dot_general(a, b, (((1,), (1,)), ((), ())), preferred_element_type=F32)


def dot_nn(a, b):
    return jnp.dot(a, b, preferred_element_type=F32)


def iota(shape, dim):
    return lax.broadcasted_iota(jnp.int32, shape, dim)


class Stream:
    def __init__(self, groups, ahead):
        self.groups = groups
        self.started = 0
        self.done = 0
        self.start_up_to(ahead)

    def start_up_to(self, count):
        while self.started < min(count, len(self.groups)):
            for copy in self.groups[self.started]:
                copy.start()
            self.started += 1

    def need(self, count):
        while self.done < count:
            for copy in self.groups[self.done]:
                copy.wait()
            self.done += 1
            self.start_up_to(self.started + 1)


def norm_kernel(hidden_hbm, gain_hbm, out_ref, hidden_ref, gain_ref, rows_ref, sem):
    copies = [
        pltpu.make_async_copy(hidden_hbm, hidden_ref, sem.at[0]),
        pltpu.make_async_copy(gain_hbm, gain_ref, sem.at[1]),
    ]
    for copy in copies:
        copy.start()
    local, steps, _ = hidden_ref.shape
    rows_ref[...] = jnp.zeros_like(rows_ref)
    for copy in copies:
        copy.wait()
    for j in range(local):
        rows_ref[pl.ds(j * steps, steps), :] = hidden_ref[j]
    rows = rows_ref[...]
    mean_square = jnp.mean(rows * rows, axis=-1, keepdims=True)
    out_ref[...] = (rows * lax.rsqrt(mean_square + 1e-06) * gain_ref[...]).astype(BF16)


def norm_rows(hidden, gain):
    width = hidden.shape[2]
    return pl.pallas_call(
        norm_kernel,
        out_shape=jax.ShapeDtypeStruct((GROUP, width), BF16),
        in_specs=[hbm(), hbm()],
        out_specs=vmem(),
        scratch_shapes=[
            pltpu.VMEM(hidden.shape, F32),
            pltpu.VMEM((1, width), F32),
            pltpu.VMEM((GROUP, width), F32),
            pltpu.SemaphoreType.DMA((2,)),
        ],
        compiler_params=pltpu.CompilerParams(vmem_limit_bytes=4 * MIB),
        name="norm_rows",
    )(far(hidden), far(gain.reshape(1, width)))


def rotated(full, cosine, sine):
    heads = full.shape[1] // HD
    parts = []
    for h in range(heads):
        one = full[:, h * HD : (h + 1) * HD]
        parts.append(one * cosine + pltpu.roll(one, HD // 2, 1) * sine)
    return jnp.concatenate(parts, axis=1)


def attention_kernel(
    local,
    steps,
    lens_ref,
    slot_req_ref,
    slot_block_ref,
    rows_ref,
    freq_ref,
    query_hbm,
    key_hbm,
    value_hbm,
    key_in,
    value_in,
    part_ref,
    key_out,
    value_out,
    weights,
    key_buf,
    value_buf,
    spread,
    new_keys,
    new_values,
    scores_buf,
    weight_buf,
    slot_max,
    slot_total,
    slot_out,
    req_max,
    req_total,
    req_out,
    weight_sem,
    in_sem,
    out_sem,
):
    pool, block, width = key_buf.shape
    heads = width // HD
    per = heads * steps
    requests = req_max.shape[0]
    groups = requests // local
    chunks = [(c, min(c + CHUNK, pool)) for c in range(0, pool, CHUNK)]

    weight_copies = [
        pltpu.make_async_copy(src, weights.at[i], weight_sem.at[i])
        for i, src in enumerate((query_hbm, key_hbm, value_hbm))
    ]

    def moves(source, target, sems, n):
        return [
            pltpu.make_async_copy(
                source.at[pl.ds(low, high - low)], target.at[pl.ds(low, high - low)], sems.at[n, i]
            )
            for i, (low, high) in enumerate(chunks)
        ]

    keys_in = moves(key_in, key_buf, in_sem, 0)
    values_in = moves(value_in, value_buf, in_sem, 1)
    keys_out = moves(key_buf, key_out, out_sem, 0)
    values_out = moves(value_buf, value_out, out_sem, 1)
    stream = Stream([[copy] for copy in weight_copies + keys_in + values_in], AHEAD)

    group_row = iota((GROUP, HD), 0)
    places = []
    for g in range(groups):
        place = group_row % steps
        for j in range(local):
            here = group_row // steps == j
            place = place + jnp.where(here, lens_ref[g * local + j], 0)
        places.append(place)
    angles = jnp.concatenate(places, axis=0).astype(F32) * freq_ref[...]
    cosine = jnp.cos(angles)
    sine = jnp.sin(angles)
    sine = jnp.where(iota(sine.shape, 1) < HD // 2, -sine, sine)

    rows = rows_ref[...]
    stream.need(1)
    queries = rotated(dot_nn(rows, weights[0]), cosine, sine).astype(BF16)
    picked = iota((requests * per, rows.shape[0]), 0)
    request, inside = picked // per, picked % per
    source = request // local * GROUP + request % local * steps + inside % steps
    choose = (source == iota(picked.shape, 1)).astype(BF16)
    wide = dot_nn(choose, queries)
    head_of = iota(wide.shape, 0) % per // steps
    spread[...] = (
        jnp.where(head_of == iota(wide.shape, 1) // HD, wide, 0.0)
        .astype(BF16)
        .reshape(requests, per, width)
    )
    stream.need(2)
    new_keys[...] = rotated(dot_nn(rows, weights[1]), cosine, sine).astype(BF16).astype(F32)
    stream.need(3)
    new_values[...] = dot_nn(rows, weights[2]).astype(BF16).astype(F32)

    patch_rows = iota((16, width), 0)

    def slot_facts(s):
        wanted = slot_req_ref[s]
        request = jnp.maximum(wanted, 0)
        base = lens_ref[request] - slot_block_ref[s] * block
        return request, jnp.where(wanted >= 0, base, -4 * block)

    def patch(buf, new, s):
        request, base = slot_facts(s)

        @pl.when((base > -steps) & (base < block))
        def _():
            first = request // local * GROUP + request % local * steps
            for t in range(steps):
                row = base + t

                @pl.when((row >= 0) & (row < block))
                def _():
                    start = pl.multiple_of(row // 16 * 16, 16)
                    hit = patch_rows == row - start
                    old = buf[s, pl.ds(start, 16), :].astype(F32)
                    fresh = new[pl.ds(first + t, 1), :]
                    buf[s, pl.ds(start, 16), :] = jnp.where(hit, fresh, old).astype(BF16)

    def patch_all(buf, new, low, high):
        def one(s, carry):
            patch(buf, new, s)
            return carry

        lax.fori_loop(low, high, one, 0)

    def pairs(low, high):
        return [(s, min(s + 2, high)) for s in range(low, high, 2)]

    for i, (low, high) in enumerate(chunks):
        stream.need(4 + i)
        patch_all(key_buf, new_keys, low, high)
        keys_out[i].start()
        for a, b in pairs(low, high):
            left = jnp.concatenate([spread[slot_facts(s)[0]] for s in range(a, b)], axis=0)
            right = key_buf[pl.ds(a, b - a)].reshape((b - a) * block, width)
            both = dot_nt(left, right)
            for s in range(a, b):
                n = s - a
                scores_buf[s] = both[n * per : (n + 1) * per, n * block : (n + 1) * block]

    scale = 1.0 / math.sqrt(HD)
    behind = iota((per, block), 1) - iota((per, block), 0) % steps
    for s in range(pool):
        allowed = behind <= slot_facts(s)[1]
        scores = jnp.where(allowed, scores_buf[s] * scale, NEG)
        top = jnp.max(scores, axis=-1, keepdims=True)
        weight = jnp.where(allowed, jnp.exp(scores - top), 0.0)
        slot_max[s] = jnp.broadcast_to(top, (per, HD))
        slot_total[s] = jnp.broadcast_to(jnp.sum(weight, axis=-1, keepdims=True), (per, HD))
        weight_buf[s] = weight.astype(BF16)

    req_max[...] = jnp.full_like(req_max, NEG)
    for s in range(pool):
        request = slot_facts(s)[0]
        req_max[request] = jnp.maximum(req_max[request], slot_max[s])

    lane_head = iota((per, HD), 0) // steps
    for i, (low, high) in enumerate(chunks):
        stream.need(4 + len(chunks) + i)
        patch_all(value_buf, new_values, low, high)
        values_out[i].start()
        for a, b in pairs(low, high):
            pieces = []
            for s in range(a, b):
                row = [jnp.zeros((per, block), BF16)] * (b - a)
                row[s - a] = weight_buf[s]
                pieces.append(jnp.concatenate(row, axis=1))
            left = jnp.concatenate(pieces, axis=0)
            mixed = dot_nn(left, value_buf[pl.ds(a, b - a)].reshape((b - a) * block, width))
            for s in range(a, b):
                mine = mixed[(s - a) * per : (s - a + 1) * per]
                result = mine[:, :HD]
                for h in range(1, heads):
                    result = jnp.where(lane_head == h, mine[:, h * HD : (h + 1) * HD], result)
                slot_out[s] = result

    for s in range(pool):
        factor = jnp.exp(slot_max[s] - req_max[slot_facts(s)[0]])
        slot_total[s] = factor * slot_total[s]
        slot_out[s] = factor * slot_out[s]
    req_total[...] = jnp.zeros_like(req_total)
    req_out[...] = jnp.zeros_like(req_out)
    for s in range(pool):
        request = slot_facts(s)[0]
        req_total[request] = req_total[request] + slot_total[s]
        req_out[request] = req_out[request] + slot_out[s]

    total = req_total[...]
    some = total > 0.0
    safe = jnp.where(some, total, 1.0)
    mean = jnp.where(some, req_out[...] / safe, 0.0).astype(BF16)
    level = jnp.where(some, req_max[...] + jnp.log(safe), NEG)
    high = level.astype(BF16).astype(F32)
    middle = (level - high).astype(BF16).astype(F32)
    low_part = (level - high - middle).astype(BF16).astype(F32)
    row = iota(level.shape, 1)
    lane = iota(level.shape, 2)
    packed = jnp.where(lane == row, high, 0.0)
    packed = packed + jnp.where(lane == row + per, middle, 0.0)
    packed = packed + jnp.where(lane == row + 2 * per, low_part, 0.0)
    packed = jnp.sum(packed, axis=1, keepdims=True)
    block_row = iota((16, HD), 0)
    for g in range(groups):
        levels = jnp.zeros((16, HD), F32)
        for j in range(local):
            b = g * local + j
            part_ref[g, pl.ds(j * per, per), :] = mean[b]
            levels = jnp.where(block_row == j, packed[b], levels)
        part_ref[g, pl.ds(local * per, 16), :] = levels.astype(BF16)
    for copy in keys_out + values_out:
        copy.wait()


def attention(rows, weights, caches, lens, slot_req, slot_block, local, steps):
    pool, block, width = caches[0].shape
    model = rows.shape[1]
    requests = lens.shape[0]
    per = width // HD * steps
    chunk_count = -(-pool // CHUNK)
    half = HD // 2
    frequency = np.power(10000.0, -np.arange(half, dtype=np.float64) * (2.0 / HD)).astype(np.float32)
    frequency = np.concatenate([frequency, frequency])[None]
    cache_shape = jax.ShapeDtypeStruct(caches[0].shape, BF16)
    slot_stat = pltpu.VMEM((pool, per, HD), F32)
    req_stat = pltpu.VMEM((requests, per, HD), F32)
    return pl.pallas_call(
        functools.partial(attention_kernel, local, steps),
        out_shape=(
            jax.ShapeDtypeStruct((requests // local, local * per + 16, HD), BF16),
            cache_shape,
            cache_shape,
        ),
        in_specs=[smem()] * 3 + [vmem()] * 2 + [hbm()] * 5,
        out_specs=(vmem(), hbm(), hbm()),
        scratch_shapes=[
            pltpu.VMEM((3, model, width), BF16),
            pltpu.VMEM((pool, block, width), BF16),
            pltpu.VMEM((pool, block, width), BF16),
            pltpu.VMEM((requests, per, width), BF16),
            pltpu.VMEM((rows.shape[0], width), F32),
            pltpu.VMEM((rows.shape[0], width), F32),
            pltpu.VMEM((pool, per, block), F32),
            pltpu.VMEM((pool, per, block), BF16),
            slot_stat,
            slot_stat,
            slot_stat,
            req_stat,
            req_stat,
            req_stat,
            pltpu.SemaphoreType.DMA((3,)),
            pltpu.SemaphoreType.DMA((2, chunk_count)),
            pltpu.SemaphoreType.DMA((2, chunk_count)),
        ],
        compiler_params=pltpu.CompilerParams(vmem_limit_bytes=40 * MIB),
        name="attention",
    )(
        far(lens),
        far(slot_req),
        far(slot_block),
        rows,
        jnp.asarray(frequency),
        *[far(array) for array in weights],
        *[far(array) for array in caches],
    )


def merge_kernel(local, steps, part_ref, weight_ref, out_ref):
    holders = part_ref.shape[0]
    width = weight_ref.shape[0]
    heads = width // HD
    per = heads * steps
    count = local * per
    values = [part_ref[g, pl.ds(0, count), :].astype(F32) for g in range(holders)]
    row = iota((count, HD), 0)
    lane = iota((count, HD), 1)
    mine = (lane % per == row % per) & (lane < 3 * per)
    levels = []
    for g in range(holders):
        stat = part_ref[g, pl.ds(count, 16), :].astype(F32)
        wide = jnp.concatenate(
            [jnp.broadcast_to(stat[j : j + 1], (per, HD)) for j in range(local)], axis=0
        )
        levels.append(jnp.sum(jnp.where(mine, wide, 0.0), axis=-1, keepdims=True))
    top = functools.reduce(jnp.maximum, levels)
    shares = [jnp.exp(level - top) for level in levels]
    total = sum(shares)
    mixed = sum(share * value for share, value in zip(shares, values))
    attended = (mixed / total).astype(BF16)
    target = iota((GROUP, count), 0)
    source = iota((GROUP, count), 1)
    parts = []
    for h in range(heads):
        pick = (source == target // steps * per + h * steps + target % steps) & (
            target < local * steps
        )
        parts.append(dot_nn(pick.astype(BF16), attended).astype(BF16))
    out_ref[...] = dot_nn(jnp.concatenate(parts, axis=1), weight_ref[...]).astype(BF16)


def merge_project(parts, out_weight, local, steps):
    return pl.pallas_call(
        functools.partial(merge_kernel, local, steps),
        out_shape=jax.ShapeDtypeStruct((GROUP, out_weight.shape[1]), BF16),
        in_specs=[vmem(), vmem()],
        out_specs=vmem(),
        compiler_params=pltpu.CompilerParams(vmem_limit_bytes=8 * MIB),
        name="merge_project",
    )(parts, out_weight)


def second_norm_kernel(hidden_ref, left_ref, right_ref, gain_ref, ids_ref, gates_ref, rows_out, res_out, rows_ref):
    local, steps, width = hidden_ref.shape
    rows_ref[...] = jnp.zeros_like(rows_ref)
    for j in range(local):
        rows_ref[pl.ds(j * steps, steps), :] = hidden_ref[j]
    residual = rows_ref[...] + (left_ref[...].astype(F32) + right_ref[...].astype(F32))
    res_out[...] = residual
    mean_square = jnp.mean(residual * residual, axis=-1, keepdims=True)
    normed = residual * lax.rsqrt(mean_square + 1e-06) * gain_ref[...]
    rows_out[:, pl.ds(0, width)] = normed.astype(BF16)
    rows_ref[:, pl.ds(0, HD)] = jnp.zeros((GROUP, HD), F32)
    lane = iota((steps, HD), 1)
    for j in range(local):
        table = jnp.zeros((steps, HD), F32)
        for k in range(ids_ref.shape[2]):
            hit = lane % EXPERTS == ids_ref[j, :, k : k + 1]
            table = table + jnp.where(hit, gates_ref[j, :, k : k + 1], 0.0)
        rows_ref[pl.ds(j * steps, steps), pl.ds(0, HD)] = table
    table = rows_ref[:, pl.ds(0, HD)]
    high = table.astype(BF16)
    low = (table - high.astype(F32)).astype(BF16)
    rows_out[:, pl.ds(width, HD)] = jnp.where(iota((GROUP, HD), 1) < EXPERTS, high.astype(F32), low.astype(F32)).astype(BF16)


def second_norm(hidden, left, right, gain, ids, gates):
    width = hidden.shape[2]
    return pl.pallas_call(
        second_norm_kernel,
        out_shape=(
            jax.ShapeDtypeStruct((GROUP, width + HD), BF16),
            jax.ShapeDtypeStruct((GROUP, width), F32),
        ),
        in_specs=[vmem()] * 6,
        out_specs=(vmem(), vmem()),
        scratch_shapes=[pltpu.VMEM((GROUP, width), F32)],
        compiler_params=pltpu.CompilerParams(vmem_limit_bytes=4 * MIB),
        name="second_norm",
    )(hidden, left, right, gain.reshape(1, width), ids, gates)


def shared_window(total, ranks):
    each = total // ranks
    length = max(-(-(r * each % 16 + each) // 16) * 16 for r in range(ranks))
    return each, length


def experts_kernel(
    tokens,
    count,
    ranks,
    rows_ref,
    gate_hbm,
    up_hbm,
    down_hbm,
    shared_gate_hbm,
    shared_up_hbm,
    shared_down_hbm,
    out_ref,
    gate_ref,
    up_ref,
    down_ref,
    inner_ref,
    total_ref,
    sem,
    shared_sem,
):
    hidden, width = gate_hbm.shape
    every = gate_ref.shape[0]
    each = hidden // count
    slim, length = shared_window(shared_gate_hbm.shape[0], ranks)
    seq_rank = lax.axis_index("seq")
    slim_low = seq_rank * slim
    slim_start = pl.multiple_of(
        jnp.minimum(slim_low // 16 * 16, shared_gate_hbm.shape[0] - length), 16
    )
    blocks = [(low, min(low + BLOCK, every)) for low in range(0, every, BLOCK)]

    def moves(source, extra, target, n):
        copies = []
        for i, (low, high) in enumerate(blocks):
            top = min(high, hidden)
            piece = [
                pltpu.make_async_copy(
                    source.at[pl.ds(low, top - low)], target.at[pl.ds(low, top - low)], sem.at[n, i]
                )
            ] if top > low else []
            if high == every:
                piece.append(
                    pltpu.make_async_copy(
                        extra.at[pl.ds(slim_start, length)],
                        target.at[pl.ds(hidden, length)],
                        shared_sem.at[n],
                    )
                )
            copies.append(piece)
        return copies

    gates = moves(gate_hbm, shared_gate_hbm, gate_ref, 0)
    ups = moves(up_hbm, shared_up_hbm, up_ref, 1)
    downs = moves(down_hbm, shared_down_hbm, down_ref, 2)
    stream = Stream([a + b for a, b in zip(gates, ups)] + downs, 2)

    first = seq_rank * count
    rows = rows_ref[:, pl.ds(0, width)]
    table = rows_ref[:, pl.ds(width, HD)]
    for i, (low, high) in enumerate(blocks):
        shape = (HD, high - low)
        unit = low + iota(shape, 1)
        expert = jnp.where(unit < hidden, first + unit // each, -1)
        share = dot_nn(table, (iota(shape, 0) % EXPERTS == expert).astype(BF16))
        if high > hidden:
            unit = low + iota(share.shape, 1) - hidden + slim_start
            mine = (unit >= slim_low) & (unit < slim_low + slim)
            in_shared = low + iota(share.shape, 1) >= hidden
            share = jnp.where(in_shared, mine.astype(F32), share)
        stream.need(i + 1)
        gate = dot_nt(rows, gate_ref[pl.ds(low, high - low), :])
        up = dot_nt(rows, up_ref[pl.ds(low, high - low), :])
        inner_ref[:, pl.ds(low, high - low)] = (jax.nn.silu(gate) * up * share).astype(BF16)

    groups = total_ref.shape[0] // GROUP
    pieces = out_ref.shape[0] // groups
    columns = width // pieces
    for i, (low, high) in enumerate(blocks):
        stream.need(len(blocks) + 1 + i)
        part = inner_ref[:, pl.ds(low, high - low)]
        for p in range(pieces):
            cut = pl.ds(p * columns, columns)
            sums = dot_nn(part, down_ref[pl.ds(low, high - low), cut])
            if i > 0:
                sums = sums + total_ref[:, cut]
            if i < len(blocks) - 1:
                total_ref[:, cut] = sums
            else:
                for g in range(groups):
                    out_ref[g * pieces + p] = sums[g * GROUP : g * GROUP + tokens].astype(BF16)


def all_experts(rows, routed, shared, tokens, pieces):
    count, each, width = routed[2].shape
    hidden = count * each
    groups = rows.shape[0] // GROUP
    every = hidden + shared_window(shared[2].shape[0], groups)[1]
    routed = [array.reshape(hidden, width) for array in routed]
    return pl.pallas_call(
        functools.partial(experts_kernel, tokens, count, groups),
        out_shape=jax.ShapeDtypeStruct((groups * pieces, tokens, width // pieces), BF16),
        in_specs=[vmem()] + [hbm()] * 6,
        out_specs=vmem(),
        scratch_shapes=[pltpu.VMEM((every, width), BF16)] * 3
        + [
            pltpu.VMEM((rows.shape[0], every), BF16),
            pltpu.VMEM((rows.shape[0], width), F32),
            pltpu.SemaphoreType.DMA((3, -(-every // BLOCK))),
            pltpu.SemaphoreType.DMA((3,)),
        ],
        compiler_params=pltpu.CompilerParams(vmem_limit_bytes=56 * MIB),
        name="experts",
    )(rows, *[far(array) for array in (*routed, *shared)])


def last_kernel(res_ref, parts_ref, out_ref):
    local, steps, columns = out_ref.shape
    total = parts_ref[0].astype(F32)
    for i in range(1, parts_ref.shape[0]):
        total = total + parts_ref[i].astype(F32)
    start = pl.multiple_of(lax.axis_index("exp") * columns, HD)
    total = total + res_ref[pl.ds(0, local * steps), pl.ds(start, columns)]
    for j in range(local):
        out_ref[j] = total[j * steps : (j + 1) * steps]


def last_sum(residual, parts, local, steps):
    return pl.pallas_call(
        last_kernel,
        out_shape=jax.ShapeDtypeStruct((local, steps, parts.shape[2]), F32),
        in_specs=[vmem(), vmem()],
        out_specs=vmem(),
        compiler_params=pltpu.CompilerParams(vmem_limit_bytes=8 * MIB),
        name="last_sum",
    )(residual, parts)


def partner(array, axis, bit):
    count = lax.axis_size(axis)
    return lax.ppermute(array, axis, [(i, i ^ bit) for i in range(count)])


def body(
    hidden_in,
    cache_lens,
    slot_request,
    slot_block,
    key_cache,
    value_cache,
    attn_gain,
    query_weight,
    key_weight,
    value_weight,
    out_weight,
    ffn_gain,
    expert_ids,
    expert_weights,
    gate_experts,
    up_experts,
    down_experts,
    gate_shared,
    up_shared,
    down_shared,
):
    local, steps, width = hidden_in.shape
    exp_count = lax.axis_size("exp")
    tokens = local * steps

    normed = norm_rows(hidden_in, attn_gain)
    rows = lax.all_gather(normed, "seq", axis=0, tiled=True)
    parts, key_out, value_out = attention(
        rows,
        (query_weight, key_weight, value_weight),
        (key_cache, value_cache),
        cache_lens,
        slot_request,
        slot_block,
        local,
        steps,
    )
    parts = lax.all_to_all(parts, "seq", split_axis=0, concat_axis=0, tiled=True)
    terms = merge_project(parts, out_weight, local, steps)
    other = partner(terms, "exp", 1)
    bit = 2
    while bit < exp_count:
        terms = (terms.astype(F32) + other.astype(F32)).astype(BF16)
        other = partner(terms, "exp", bit)
        bit *= 2
    ffn_in, residual = second_norm(
        hidden_in, terms, other, ffn_gain, expert_ids, expert_weights
    )
    all_rows = lax.all_gather(ffn_in, "seq", axis=0, tiled=True)
    sums = all_experts(
        all_rows,
        (jnp.swapaxes(gate_experts, 1, 2), jnp.swapaxes(up_experts, 1, 2), down_experts),
        (jnp.swapaxes(gate_shared, 0, 1), jnp.swapaxes(up_shared, 0, 1), down_shared),
        tokens,
        exp_count,
    )
    sums = lax.all_to_all(sums, ("seq", "exp"), split_axis=0, concat_axis=0, tiled=True)
    hidden_out = last_sum(residual, sums, local, steps)
    return hidden_out, key_out, value_out


def solution(mesh):
    in_specs = (
        P("seq", None, None),
        P(),
        P("seq"),
        P("seq"),
        P("seq", None, "exp"),
        P("seq", None, "exp"),
        P(),
        P(None, "exp"),
        P(None, "exp"),
        P(None, "exp"),
        P("exp", None),
        P(),
        P("seq", None, None),
        P("seq", None, None),
        P("seq", None, "exp"),
        P("seq", None, "exp"),
        P("seq", "exp", None),
        P(None, "exp"),
        P(None, "exp"),
        P("exp", None),
    )
    out_specs = (P("seq", None, "exp"), P("seq", None, "exp"), P("seq", None, "exp"))
    return jax.shard_map(body, mesh=mesh, in_specs=in_specs, out_specs=out_specs, check_vma=False)
```

```python
import functools
import math

import jax
import jax.numpy as jnp
import numpy as np
from jax import lax
from jax.experimental import pallas as pl
from jax.experimental.pallas import tpu as pltpu
from jax.sharding import PartitionSpec as P

HD = 128
EXPERTS = 64
GROUP = 16
BLOCK = 768
FETCHED = 2
AHEAD = 3
CHUNK = 16
NEG = -1e30
MIB = 1 << 20
F32 = jnp.float32
BF16 = jnp.bfloat16


def vmem():
    return pl.BlockSpec(memory_space=pltpu.VMEM)


def smem():
    return pl.BlockSpec(memory_space=pltpu.SMEM)


def hbm():
    return pl.BlockSpec(memory_space=pl.ANY)


def far(array):
    return pltpu.with_memory_space_constraint(array, pltpu.HBM)


def near(array):
    return pltpu.with_memory_space_constraint(array, pltpu.VMEM)


def dot_nt(a, b):
    return lax.dot_general(a, b, (((1,), (1,)), ((), ())), preferred_element_type=F32)


def dot_nn(a, b):
    return jnp.dot(a, b, preferred_element_type=F32)


def iota(shape, dim):
    return lax.broadcasted_iota(jnp.int32, shape, dim)


class Stream:
    def __init__(self, groups, ahead):
        self.groups = groups
        self.started = 0
        self.done = 0
        self.start_up_to(ahead)

    def start_up_to(self, count):
        while self.started < min(count, len(self.groups)):
            for copy in self.groups[self.started]:
                copy.start()
            self.started += 1

    def need(self, count):
        while self.done < count:
            for copy in self.groups[self.done]:
                copy.wait()
            self.done += 1
            self.start_up_to(self.started + 1)


def norm_kernel(hidden_hbm, gain_hbm, out_ref, hidden_ref, gain_ref, rows_ref, sem):
    copies = [
        pltpu.make_async_copy(hidden_hbm, hidden_ref, sem.at[0]),
        pltpu.make_async_copy(gain_hbm, gain_ref, sem.at[1]),
    ]
    for copy in copies:
        copy.start()
    local, steps, _ = hidden_ref.shape
    rows_ref[...] = jnp.zeros_like(rows_ref)
    for copy in copies:
        copy.wait()
    for j in range(local):
        rows_ref[pl.ds(j * steps, steps), :] = hidden_ref[j]
    rows = rows_ref[...]
    mean_square = jnp.mean(rows * rows, axis=-1, keepdims=True)
    out_ref[...] = (rows * lax.rsqrt(mean_square + 1e-06) * gain_ref[...]).astype(BF16)


def norm_rows(hidden, gain):
    width = hidden.shape[2]
    return pl.pallas_call(
        norm_kernel,
        out_shape=jax.ShapeDtypeStruct((GROUP, width), BF16),
        in_specs=[hbm(), hbm()],
        out_specs=vmem(),
        scratch_shapes=[
            pltpu.VMEM(hidden.shape, F32),
            pltpu.VMEM((1, width), F32),
            pltpu.VMEM((GROUP, width), F32),
            pltpu.SemaphoreType.DMA((2,)),
        ],
        compiler_params=pltpu.CompilerParams(vmem_limit_bytes=4 * MIB),
        name="norm_rows",
    )(far(hidden), far(gain.reshape(1, width)))


def rotated(full, cosine, sine):
    heads = full.shape[1] // HD
    parts = []
    for h in range(heads):
        one = full[:, h * HD : (h + 1) * HD]
        parts.append(one * cosine + pltpu.roll(one, HD // 2, 1) * sine)
    return jnp.concatenate(parts, axis=1)


def rotation(lens_ref, groups, local, steps):
    group_row = iota((GROUP, HD), 0)
    places = []
    for g in range(groups):
        place = group_row % steps
        for j in range(local):
            here = group_row // steps == j
            place = place + jnp.where(here, lens_ref[g * local + j], 0)
        places.append(place)
    half = HD // 2
    lane = iota((1, HD), 1) % half
    frequency = jnp.zeros((1, HD), F32)
    for i in range(half):
        frequency = jnp.where(lane == i, float(np.float32(10000.0 ** (-i / half))), frequency)
    angles = jnp.concatenate(places, axis=0).astype(F32) * frequency
    sine = jnp.sin(angles)
    return jnp.cos(angles), jnp.where(iota(sine.shape, 1) < half, -sine, sine)


def spread_heads(queries, requests, local, steps):
    per = queries.shape[1] // HD * steps
    picked = iota((requests * per, queries.shape[0]), 0)
    request, inside = picked // per, picked % per
    source = request // local * GROUP + request % local * steps + inside % steps
    choose = (source == iota(picked.shape, 1)).astype(BF16)
    wide = dot_nn(choose, queries)
    head_of = iota(wide.shape, 0) % per // steps
    return jnp.where(head_of == iota(wide.shape, 1) // HD, wide, 0.0).astype(BF16)


def own_head(mixed, steps):
    rows, width = mixed.shape
    heads = width // HD
    head = iota((rows, HD), 0) % (heads * steps) // steps
    result = mixed[:, :HD]
    for h in range(1, heads):
        result = jnp.where(head == h, mixed[:, h * HD : (h + 1) * HD], result)
    return result


def slot_place(lens_ref, slot_req_ref, slot_block_ref, s, block):
    wanted = slot_req_ref[s]
    request = jnp.maximum(wanted, 0)
    base = lens_ref[request] - slot_block_ref[s] * block
    return request, jnp.where(wanted >= 0, base, -4 * block)


def patch_slots(slot_facts, local, steps, buf, new, low, high):
    _, block, width = buf.shape
    patch_rows = iota((16, width), 0)

    def one(s, carry):
        request, base = slot_facts(s)

        @pl.when((base > -steps) & (base < block))
        def _():
            first = request // local * GROUP + request % local * steps
            for t in range(steps):
                row = base + t

                @pl.when((row >= 0) & (row < block))
                def _():
                    start = pl.multiple_of(row // 16 * 16, 16)
                    hit = patch_rows == row - start
                    old = buf[s, pl.ds(start, 16), :].astype(F32)
                    fresh = new[pl.ds(first + t, 1), :]
                    buf[s, pl.ds(start, 16), :] = jnp.where(hit, fresh, old).astype(BF16)

        return carry

    lax.fori_loop(low, high, one, 0)


def attention_kernel(
    local,
    steps,
    lens_ref,
    slot_req_ref,
    slot_block_ref,
    rows_ref,
    query_hbm,
    key_in,
    value_in,
    part_ref,
    queries_ref,
    weight,
    key_buf,
    value_buf,
    spread,
    scores_buf,
    weight_buf,
    slot_max,
    slot_total,
    slot_out,
    req_max,
    req_total,
    req_out,
    weight_sem,
    in_sem,
):
    pool, block, width = key_buf.shape
    heads = width // HD
    per = heads * steps
    requests = req_max.shape[0]
    groups = requests // local
    chunks = [(c, min(c + CHUNK, pool)) for c in range(0, pool, CHUNK)]

    weight_copy = pltpu.make_async_copy(query_hbm, weight, weight_sem.at[0])

    def moves(source, target, sems, n):
        return [
            pltpu.make_async_copy(
                source.at[pl.ds(low, high - low)], target.at[pl.ds(low, high - low)], sems.at[n, i]
            )
            for i, (low, high) in enumerate(chunks)
        ]

    keys_in = moves(key_in, key_buf, in_sem, 0)
    values_in = moves(value_in, value_buf, in_sem, 1)
    stream = Stream([[copy] for copy in [weight_copy] + keys_in + values_in], AHEAD)

    cosine, sine = rotation(lens_ref, groups, local, steps)
    stream.need(1)
    queries = rotated(dot_nn(rows_ref[...], weight[...]), cosine, sine).astype(BF16)
    queries_ref[...] = queries
    spread[...] = spread_heads(queries, requests, local, steps).reshape(requests, per, width)

    def slot_facts(s):
        return slot_place(lens_ref, slot_req_ref, slot_block_ref, s, block)

    def pairs(low, high):
        return [(s, min(s + 2, high)) for s in range(low, high, 2)]

    for i, (low, high) in enumerate(chunks):
        stream.need(2 + i)
        for a, b in pairs(low, high):
            left = jnp.concatenate([spread[slot_facts(s)[0]] for s in range(a, b)], axis=0)
            right = key_buf[pl.ds(a, b - a)].reshape((b - a) * block, width)
            both = dot_nt(left, right)
            for s in range(a, b):
                n = s - a
                scores_buf[s] = both[n * per : (n + 1) * per, n * block : (n + 1) * block]

    scale = 1.0 / math.sqrt(HD)
    position = iota((per, block), 1)
    for s in range(pool):
        allowed = position < slot_facts(s)[1]
        scores = jnp.where(allowed, scores_buf[s] * scale, NEG)
        top = jnp.max(scores, axis=-1, keepdims=True)
        weight = jnp.where(allowed, jnp.exp(scores - top), 0.0)
        slot_max[s] = jnp.broadcast_to(top, (per, HD))
        slot_total[s] = jnp.broadcast_to(jnp.sum(weight, axis=-1, keepdims=True), (per, HD))
        weight_buf[s] = weight.astype(BF16)

    req_max[...] = jnp.full_like(req_max, NEG)
    for s in range(pool):
        request = slot_facts(s)[0]
        req_max[request] = jnp.maximum(req_max[request], slot_max[s])

    for i, (low, high) in enumerate(chunks):
        stream.need(2 + len(chunks) + i)
        for a, b in pairs(low, high):
            pieces = []
            for s in range(a, b):
                row = [jnp.zeros((per, block), BF16)] * (b - a)
                row[s - a] = weight_buf[s]
                pieces.append(jnp.concatenate(row, axis=1))
            left = jnp.concatenate(pieces, axis=0)
            mixed = dot_nn(left, value_buf[pl.ds(a, b - a)].reshape((b - a) * block, width))
            for s in range(a, b):
                slot_out[s] = own_head(mixed[(s - a) * per : (s - a + 1) * per], steps)

    for s in range(pool):
        factor = jnp.exp(slot_max[s] - req_max[slot_facts(s)[0]])
        slot_total[s] = factor * slot_total[s]
        slot_out[s] = factor * slot_out[s]
    req_total[...] = jnp.zeros_like(req_total)
    req_out[...] = jnp.zeros_like(req_out)
    for s in range(pool):
        request = slot_facts(s)[0]
        req_total[request] = req_total[request] + slot_total[s]
        req_out[request] = req_out[request] + slot_out[s]

    total = req_total[...]
    some = total > 0.0
    safe = jnp.where(some, total, 1.0)
    mean = jnp.where(some, req_out[...] / safe, 0.0).astype(BF16)
    level = jnp.where(some, req_max[...] + jnp.log(safe), NEG)
    high = level.astype(BF16).astype(F32)
    middle = (level - high).astype(BF16).astype(F32)
    low_part = (level - high - middle).astype(BF16).astype(F32)
    row = iota(level.shape, 1)
    lane = iota(level.shape, 2)
    packed = jnp.where(lane == row, high, 0.0)
    packed = packed + jnp.where(lane == row + per, middle, 0.0)
    packed = packed + jnp.where(lane == row + 2 * per, low_part, 0.0)
    packed = jnp.sum(packed, axis=1, keepdims=True)
    block_row = iota((16, HD), 0)
    for g in range(groups):
        levels = jnp.zeros((16, HD), F32)
        for j in range(local):
            b = g * local + j
            part_ref[g, pl.ds(j * per, per), :] = mean[b]
            levels = jnp.where(block_row == j, packed[b], levels)
        part_ref[g, pl.ds(local * per, 16), :] = levels.astype(BF16)


def attention(rows, weight, caches, lens, slot_req, slot_block, local, steps):
    pool, block, width = caches[0].shape
    model = rows.shape[1]
    requests = lens.shape[0]
    per = width // HD * steps
    chunk_count = -(-pool // CHUNK)
    new_shape = jax.ShapeDtypeStruct((rows.shape[0], width), BF16)
    slot_stat = pltpu.VMEM((pool, per, HD), F32)
    req_stat = pltpu.VMEM((requests, per, HD), F32)
    return pl.pallas_call(
        functools.partial(attention_kernel, local, steps),
        out_shape=(
            jax.ShapeDtypeStruct((requests // local, local * per + 16, HD), BF16),
            new_shape,
        ),
        in_specs=[smem()] * 3 + [vmem()] + [hbm()] * 3,
        out_specs=(vmem(), vmem()),
        scratch_shapes=[
            pltpu.VMEM((model, width), BF16),
            pltpu.VMEM((pool, block, width), BF16),
            pltpu.VMEM((pool, block, width), BF16),
            pltpu.VMEM((requests, per, width), BF16),
            pltpu.VMEM((pool, per, block), F32),
            pltpu.VMEM((pool, per, block), BF16),
            slot_stat,
            slot_stat,
            slot_stat,
            req_stat,
            req_stat,
            req_stat,
            pltpu.SemaphoreType.DMA((1,)),
            pltpu.SemaphoreType.DMA((2, chunk_count)),
        ],
        compiler_params=pltpu.CompilerParams(vmem_limit_bytes=28 * MIB),
        name="attention",
    )(
        far(lens),
        far(slot_req),
        far(slot_block),
        rows,
        far(weight),
        *[far(array) for array in caches],
    )


def fresh_kernel(
    local,
    steps,
    lens_ref,
    rows_ref,
    queries_ref,
    key_hbm,
    value_hbm,
    keys_ref,
    values_ref,
    mean_ref,
    level_ref,
    weights,
    sem,
):
    copies = [
        pltpu.make_async_copy(source, weights.at[n], sem.at[n])
        for n, source in enumerate((key_hbm, value_hbm))
    ]
    for copy in copies:
        copy.start()
    groups = rows_ref.shape[0] // GROUP
    width = keys_ref.shape[1]
    per = width // HD * steps
    own = pl.ds(pl.multiple_of(lax.axis_index("seq") * GROUP, GROUP), GROUP)
    spread = spread_heads(queries_ref[own, :], local, local, steps)
    cosine, sine = rotation(lens_ref, groups, local, steps)
    rows = rows_ref[...]
    for copy in copies:
        copy.wait()
    keys_ref[...] = rotated(dot_nn(rows, weights[0]), cosine, sine).astype(BF16)
    values_ref[...] = dot_nn(rows, weights[1]).astype(BF16)
    scores = dot_nt(spread, keys_ref[own, :]) * (1.0 / math.sqrt(HD))
    row = iota(scores.shape, 0)
    column = iota(scores.shape, 1)
    allowed = (column // steps == row // per) & (column % steps <= row % steps)
    scores = jnp.where(allowed, scores, NEG)
    top = jnp.max(scores, axis=-1, keepdims=True)
    weight = jnp.where(allowed, jnp.exp(scores - top), 0.0)
    total = jnp.sum(weight, axis=-1, keepdims=True)
    mixed = own_head(dot_nn(weight.astype(BF16), values_ref[own, :]), steps)
    mean_ref[...] = mixed / total
    level_ref[...] = jnp.broadcast_to(top + jnp.log(total), level_ref.shape)


def fresh_rows(rows, queries, weights, lens, local, steps):
    model, width = weights[0].shape
    count = local * (width // HD) * steps
    new_shape = jax.ShapeDtypeStruct((rows.shape[0], width), BF16)
    own_shape = jax.ShapeDtypeStruct((count, HD), F32)
    return pl.pallas_call(
        functools.partial(fresh_kernel, local, steps),
        out_shape=(new_shape, new_shape, own_shape, own_shape),
        in_specs=[smem()] + [vmem()] * 2 + [hbm()] * 2,
        out_specs=(vmem(),) * 4,
        scratch_shapes=[pltpu.VMEM((2, model, width), BF16), pltpu.SemaphoreType.DMA((2,))],
        compiler_params=pltpu.CompilerParams(vmem_limit_bytes=12 * MIB),
        cost_estimate=pl.CostEstimate(
            flops=4 * rows.shape[0] * model * width,
            bytes_accessed=4 * model * width,
            transcendentals=0,
        ),
        name="fresh_rows",
    )(far(lens), rows, queries, *[far(array) for array in weights])


def cache_kernel(
    local,
    steps,
    lens_ref,
    slot_req_ref,
    slot_block_ref,
    keys_ref,
    values_ref,
    _,
    key_in,
    value_in,
    key_out,
    value_out,
    new_keys,
    new_values,
    key_buf,
    value_buf,
    in_sem,
    out_sem,
):
    pool, block, _ = key_in.shape
    cuts = [(low, min(low + CHUNK, pool)) for low in range(0, pool, CHUNK)]
    caches = ((key_in, key_buf, key_out, new_keys), (value_in, value_buf, value_out, new_values))
    steps_of = [(n, i) for n in range(2) for i in range(len(cuts))]

    def move(source, target, sem, n, i):
        low, high = cuts[i]
        span = pl.ds(low, high - low)
        return pltpu.make_async_copy(source.at[span], target.at[span], sem.at[n, i])

    stream = Stream([[move(caches[n][0], caches[n][1], in_sem, n, i)] for n, i in steps_of], AHEAD)
    outs = [move(caches[n][1], caches[n][2], out_sem, n, i) for n, i in steps_of]
    new_keys[...] = keys_ref[...].astype(F32)
    new_values[...] = values_ref[...].astype(F32)

    def slot_facts(s):
        return slot_place(lens_ref, slot_req_ref, slot_block_ref, s, block)

    for k, (n, i) in enumerate(steps_of):
        stream.need(k + 1)
        patch_slots(slot_facts, local, steps, caches[n][1], caches[n][3], *cuts[i])
        outs[k].start()
    for copy in outs:
        copy.wait()


def updated_caches(caches, keys, values, lens, slot_req, slot_block, after, local, steps):
    pool, block, width = caches[0].shape
    cache_shape = jax.ShapeDtypeStruct(caches[0].shape, BF16)
    return pl.pallas_call(
        functools.partial(cache_kernel, local, steps),
        out_shape=(cache_shape, cache_shape),
        in_specs=[smem()] * 3 + [vmem()] * 2 + [hbm()] * 3,
        out_specs=(hbm(), hbm()),
        scratch_shapes=[pltpu.VMEM(keys.shape, F32)] * 2
        + [pltpu.VMEM((pool, block, width), BF16)] * 2
        + [pltpu.SemaphoreType.DMA((2, -(-pool // CHUNK)))] * 2,
        compiler_params=pltpu.CompilerParams(vmem_limit_bytes=20 * MIB),
        cost_estimate=pl.CostEstimate(
            flops=0, bytes_accessed=4 * 2 * pool * block * width, transcendentals=0
        ),
        name="updated_caches",
    )(far(lens), far(slot_req), far(slot_block), keys, values, after, *[far(array) for array in caches])


def merge_kernel(local, steps, part_ref, mean_ref, level_ref, weight_ref, out_ref):
    holders = part_ref.shape[0]
    width = weight_ref.shape[0]
    heads = width // HD
    per = heads * steps
    count = local * per
    values = [part_ref[g, pl.ds(0, count), :].astype(F32) for g in range(holders)]
    row = iota((count, HD), 0)
    lane = iota((count, HD), 1)
    mine = (lane % per == row % per) & (lane < 3 * per)
    levels = []
    for g in range(holders):
        stat = part_ref[g, pl.ds(count, 16), :].astype(F32)
        wide = jnp.concatenate(
            [jnp.broadcast_to(stat[j : j + 1], (per, HD)) for j in range(local)], axis=0
        )
        levels.append(jnp.sum(jnp.where(mine, wide, 0.0), axis=-1, keepdims=True))
    values.append(mean_ref[...])
    levels.append(level_ref[:, :1])
    top = functools.reduce(jnp.maximum, levels)
    shares = [jnp.exp(level - top) for level in levels]
    total = sum(shares)
    mixed = sum(share * value for share, value in zip(shares, values))
    attended = (mixed / total).astype(BF16)
    target = iota((GROUP, count), 0)
    source = iota((GROUP, count), 1)
    parts = []
    for h in range(heads):
        pick = (source == target // steps * per + h * steps + target % steps) & (
            target < local * steps
        )
        parts.append(dot_nn(pick.astype(BF16), attended).astype(BF16))
    out_ref[...] = dot_nn(jnp.concatenate(parts, axis=1), weight_ref[...]).astype(BF16)


def merge_project(parts, mean, level, out_weight, local, steps):
    return pl.pallas_call(
        functools.partial(merge_kernel, local, steps),
        out_shape=jax.ShapeDtypeStruct((GROUP, out_weight.shape[1]), BF16),
        in_specs=[vmem()] * 4,
        out_specs=vmem(),
        compiler_params=pltpu.CompilerParams(vmem_limit_bytes=8 * MIB),
        name="merge_project",
    )(parts, mean, level, out_weight)


def second_norm_kernel(hidden_ref, left_ref, right_ref, gain_ref, ids_ref, gates_ref, rows_out, res_out, rows_ref):
    local, steps, width = hidden_ref.shape
    rows_ref[...] = jnp.zeros_like(rows_ref)
    for j in range(local):
        rows_ref[pl.ds(j * steps, steps), :] = hidden_ref[j]
    residual = rows_ref[...] + (left_ref[...].astype(F32) + right_ref[...].astype(F32))
    res_out[...] = residual
    mean_square = jnp.mean(residual * residual, axis=-1, keepdims=True)
    normed = residual * lax.rsqrt(mean_square + 1e-06) * gain_ref[...]
    rows_out[:, pl.ds(0, width)] = normed.astype(BF16)
    rows_ref[:, pl.ds(0, HD)] = jnp.zeros((GROUP, HD), F32)
    lane = iota((steps, HD), 1)
    for j in range(local):
        table = jnp.zeros((steps, HD), F32)
        for k in range(ids_ref.shape[2]):
            hit = lane % EXPERTS == ids_ref[j, :, k : k + 1]
            table = table + jnp.where(hit, gates_ref[j, :, k : k + 1], 0.0)
        rows_ref[pl.ds(j * steps, steps), pl.ds(0, HD)] = table
    table = rows_ref[:, pl.ds(0, HD)]
    high = table.astype(BF16)
    low = (table - high.astype(F32)).astype(BF16)
    rows_out[:, pl.ds(width, HD)] = jnp.where(iota((GROUP, HD), 1) < EXPERTS, high.astype(F32), low.astype(F32)).astype(BF16)


def second_norm(hidden, left, right, gain, ids, gates):
    width = hidden.shape[2]
    return pl.pallas_call(
        second_norm_kernel,
        out_shape=(
            jax.ShapeDtypeStruct((GROUP, width + HD), BF16),
            jax.ShapeDtypeStruct((GROUP, width), F32),
        ),
        in_specs=[vmem()] * 6,
        out_specs=(vmem(), vmem()),
        scratch_shapes=[pltpu.VMEM((GROUP, width), F32)],
        compiler_params=pltpu.CompilerParams(vmem_limit_bytes=4 * MIB),
        name="second_norm",
    )(hidden, left, right, gain.reshape(1, width), ids, gates)


def shared_window(total, ranks):
    each = total // ranks
    length = max(-(-(r * each % 16 + each) // 16) * 16 for r in range(ranks))
    return each, length


def expert_blocks(hidden, every):
    blocks = [(low, min(low + BLOCK, every)) for low in range(0, every, BLOCK)]
    return blocks, min(FETCHED, sum(high <= hidden for _, high in blocks))


def fetch_kernel(low, rows, _, gate_hbm, up_hbm, gate_ref, up_ref, sem):
    copies = [
        pltpu.make_async_copy(source.at[pl.ds(low, rows)], target, sem.at[n])
        for n, (source, target) in enumerate(((gate_hbm, gate_ref), (up_hbm, up_ref)))
    ]
    for copy in copies:
        copy.start()
    for copy in copies:
        copy.wait()


def fetch(block, gate, up, after):
    low, high = block
    shape = pltpu.VMEM((high - low, gate.shape[1]), BF16)
    return pl.pallas_call(
        functools.partial(fetch_kernel, low, high - low),
        out_shape=(shape, shape),
        in_specs=[hbm()] * 3,
        out_specs=(vmem(), vmem()),
        scratch_shapes=[pltpu.SemaphoreType.DMA((2,))],
        compiler_params=pltpu.CompilerParams(vmem_limit_bytes=MIB),
        cost_estimate=pl.CostEstimate(
            flops=0, bytes_accessed=4 * (high - low) * gate.shape[1], transcendentals=0
        ),
        name="fetch_weights",
    )(after, far(gate), far(up))


def experts_kernel(
    tokens,
    count,
    ranks,
    fetched,
    rows_ref,
    *refs,
):
    early = [(refs[2 * i], refs[2 * i + 1]) for i in range(fetched)]
    streamed_experts(tokens, count, ranks, early, rows_ref, *refs[2 * fetched :])


def streamed_experts(
    tokens,
    count,
    ranks,
    early,
    rows_ref,
    gate_hbm,
    up_hbm,
    down_hbm,
    shared_gate_hbm,
    shared_up_hbm,
    shared_down_hbm,
    out_ref,
    gate_ref,
    up_ref,
    down_ref,
    inner_ref,
    total_ref,
    sem,
    shared_sem,
):
    hidden, width = gate_hbm.shape
    every = down_ref.shape[0]
    each = hidden // count
    slim, length = shared_window(shared_gate_hbm.shape[0], ranks)
    seq_rank = lax.axis_index("seq")
    slim_low = seq_rank * slim
    slim_start = pl.multiple_of(
        jnp.minimum(slim_low // 16 * 16, shared_gate_hbm.shape[0] - length), 16
    )
    blocks, _ = expert_blocks(hidden, every)
    skipped = blocks[len(early) - 1][1] if early else 0

    def moves(source, extra, target, n, skip):
        copies = []
        for i, (low, high) in enumerate(blocks):
            top = min(high, hidden)
            piece = []
            if low < skip:
                continue
            if top > low:
                piece.append(
                    pltpu.make_async_copy(
                        source.at[pl.ds(low, top - low)],
                        target.at[pl.ds(low - skip, top - low)],
                        sem.at[n, i],
                    )
                )
            if high == every:
                piece.append(
                    pltpu.make_async_copy(
                        extra.at[pl.ds(slim_start, length)],
                        target.at[pl.ds(hidden - skip, length)],
                        shared_sem.at[n],
                    )
                )
            copies.append(piece)
        return copies

    gates = moves(gate_hbm, shared_gate_hbm, gate_ref, 0, skipped)
    ups = moves(up_hbm, shared_up_hbm, up_ref, 1, skipped)
    downs = moves(down_hbm, shared_down_hbm, down_ref, 2, 0)
    stream = Stream([a + b for a, b in zip(gates, ups)] + downs, 2)

    first = seq_rank * count
    rows = rows_ref[:, pl.ds(0, width)]
    table = rows_ref[:, pl.ds(width, HD)]
    for i, (low, high) in enumerate(blocks):
        shape = (HD, high - low)
        unit = low + iota(shape, 1)
        expert = jnp.where(unit < hidden, first + unit // each, -1)
        share = dot_nn(table, (iota(shape, 0) % EXPERTS == expert).astype(BF16))
        if high > hidden:
            unit = low + iota(share.shape, 1) - hidden + slim_start
            mine = (unit >= slim_low) & (unit < slim_low + slim)
            in_shared = low + iota(share.shape, 1) >= hidden
            share = jnp.where(in_shared, mine.astype(F32), share)
        if i < len(early):
            gate_block, up_block = (ref[...] for ref in early[i])
        else:
            stream.need(i + 1 - len(early))
            gate_block = gate_ref[pl.ds(low - skipped, high - low), :]
            up_block = up_ref[pl.ds(low - skipped, high - low), :]
        gate = dot_nt(rows, gate_block)
        up = dot_nt(rows, up_block)
        inner_ref[:, pl.ds(low, high - low)] = (jax.nn.silu(gate) * up * share).astype(BF16)

    groups = total_ref.shape[0] // GROUP
    pieces = out_ref.shape[0] // groups
    columns = width // pieces
    for i, (low, high) in enumerate(blocks):
        stream.need(len(gates) + 1 + i)
        part = inner_ref[:, pl.ds(low, high - low)]
        for p in range(pieces):
            cut = pl.ds(p * columns, columns)
            sums = dot_nn(part, down_ref[pl.ds(low, high - low), cut])
            if i > 0:
                sums = sums + total_ref[:, cut]
            if i < len(blocks) - 1:
                total_ref[:, cut] = sums
            else:
                for g in range(groups):
                    out_ref[g * pieces + p] = sums[g * GROUP : g * GROUP + tokens].astype(BF16)


def all_experts(rows, early, routed, shared, tokens, pieces):
    count, each, width = routed[2].shape
    hidden = count * each
    groups = rows.shape[0] // GROUP
    every = hidden + shared_window(shared[2].shape[0], groups)[1]
    routed = [array.reshape(hidden, width) for array in routed]
    early = [array for pair in early for array in pair]
    rest = every - sum(array.shape[0] for array in early) // 2
    return pl.pallas_call(
        functools.partial(experts_kernel, tokens, count, groups, len(early) // 2),
        out_shape=jax.ShapeDtypeStruct((groups * pieces, tokens, width // pieces), BF16),
        in_specs=[vmem()] * (1 + len(early)) + [hbm()] * 6,
        out_specs=vmem(),
        scratch_shapes=[pltpu.VMEM((rest, width), BF16)] * 2
        + [
            pltpu.VMEM((every, width), BF16),
            pltpu.VMEM((rows.shape[0], every), BF16),
            pltpu.VMEM((rows.shape[0], width), F32),
            pltpu.SemaphoreType.DMA((3, -(-every // BLOCK))),
            pltpu.SemaphoreType.DMA((3,)),
        ],
        compiler_params=pltpu.CompilerParams(
            vmem_limit_bytes=(2 * rest + every) * width * 2 + 8 * MIB
        ),
        name="experts",
    )(rows, *[near(array) for array in early], *[far(array) for array in (*routed, *shared)])


def last_kernel(res_ref, parts_ref, out_ref):
    local, steps, columns = out_ref.shape
    total = parts_ref[0].astype(F32)
    for i in range(1, parts_ref.shape[0]):
        total = total + parts_ref[i].astype(F32)
    start = pl.multiple_of(lax.axis_index("exp") * columns, HD)
    total = total + res_ref[pl.ds(0, local * steps), pl.ds(start, columns)]
    for j in range(local):
        out_ref[j] = total[j * steps : (j + 1) * steps]


def last_sum(residual, parts, local, steps):
    return pl.pallas_call(
        last_kernel,
        out_shape=jax.ShapeDtypeStruct((local, steps, parts.shape[2]), F32),
        in_specs=[vmem(), vmem()],
        out_specs=vmem(),
        compiler_params=pltpu.CompilerParams(vmem_limit_bytes=8 * MIB),
        name="last_sum",
    )(residual, parts)


def partner(array, axis, bit):
    count = lax.axis_size(axis)
    return lax.ppermute(array, axis, [(i, i ^ bit) for i in range(count)])


def body(
    hidden_in,
    cache_lens,
    slot_request,
    slot_block,
    key_cache,
    value_cache,
    attn_gain,
    query_weight,
    key_weight,
    value_weight,
    out_weight,
    ffn_gain,
    expert_ids,
    expert_weights,
    gate_experts,
    up_experts,
    down_experts,
    gate_shared,
    up_shared,
    down_shared,
):
    local, steps, width = hidden_in.shape
    exp_count = lax.axis_size("exp")
    tokens = local * steps

    normed = norm_rows(hidden_in, attn_gain)
    rows = lax.all_gather(normed, "seq", axis=0, tiled=True)
    parts, queries = attention(
        rows,
        query_weight,
        (key_cache, value_cache),
        cache_lens,
        slot_request,
        slot_block,
        local,
        steps,
    )
    parts = lax.all_to_all(parts, "seq", split_axis=0, concat_axis=0, tiled=True)
    new_keys, new_values, mean, level = fresh_rows(
        rows, queries, (key_weight, value_weight), cache_lens, local, steps
    )
    terms = merge_project(parts, mean, level, out_weight, local, steps)
    gate_rows = jnp.swapaxes(gate_experts, 1, 2).reshape(-1, width)
    up_rows = jnp.swapaxes(up_experts, 1, 2).reshape(-1, width)
    hidden = gate_rows.shape[0]
    extra = shared_window(down_shared.shape[0], lax.axis_size("seq"))[1]
    blocks, fetched = expert_blocks(hidden, hidden + extra)
    early = []
    other = partner(terms, "exp", 1)
    bit = 2
    while bit < exp_count:
        if len(early) < fetched:
            early.append(fetch(blocks[len(early)], gate_rows, up_rows, terms))
            other, early[-1] = lax.optimization_barrier((other, early[-1]))
        terms = (terms.astype(F32) + other.astype(F32)).astype(BF16)
        other = partner(terms, "exp", bit)
        bit *= 2
    while len(early) < fetched:
        early.append(fetch(blocks[len(early)], gate_rows, up_rows, terms))
    ffn_in, residual = second_norm(
        hidden_in, terms, other, ffn_gain, expert_ids, expert_weights
    )
    all_rows = lax.all_gather(ffn_in, "seq", axis=0, tiled=True)
    sums = all_experts(
        all_rows,
        early,
        (jnp.swapaxes(gate_experts, 1, 2), jnp.swapaxes(up_experts, 1, 2), down_experts),
        (jnp.swapaxes(gate_shared, 0, 1), jnp.swapaxes(up_shared, 0, 1), down_shared),
        tokens,
        exp_count,
    )
    key_out, value_out = updated_caches(
        (key_cache, value_cache),
        new_keys,
        new_values,
        cache_lens,
        slot_request,
        slot_block,
        sums,
        local,
        steps,
    )
    sums = lax.all_to_all(sums, ("seq", "exp"), split_axis=0, concat_axis=0, tiled=True)
    hidden_out = last_sum(residual, sums, local, steps)
    return hidden_out, key_out, value_out


def solution(mesh):
    in_specs = (
        P("seq", None, None),
        P(),
        P("seq"),
        P("seq"),
        P("seq", None, "exp"),
        P("seq", None, "exp"),
        P(),
        P(None, "exp"),
        P(None, "exp"),
        P(None, "exp"),
        P("exp", None),
        P(),
        P("seq", None, None),
        P("seq", None, None),
        P("seq", None, "exp"),
        P("seq", None, "exp"),
        P("seq", "exp", None),
        P(None, "exp"),
        P(None, "exp"),
        P("exp", None),
    )
    out_specs = (P("seq", None, "exp"), P("seq", None, "exp"), P("seq", None, "exp"))
    return jax.shard_map(body, mesh=mesh, in_specs=in_specs, out_specs=out_specs, check_vma=False)
```

```python
import functools
import math

import jax
import jax.numpy as jnp
import numpy as np
from jax import lax
from jax.experimental import pallas as pl
from jax.experimental.pallas import tpu as pltpu
from jax.sharding import PartitionSpec as P

HD = 128
EXPERTS = 64
GROUP = 16
BLOCK = 768
FETCHED = 2
AHEAD = 2
CHUNK = 46
NEG = -1e30
MIB = 1 << 20
F32 = jnp.float32
BF16 = jnp.bfloat16


def vmem():
    return pl.BlockSpec(memory_space=pltpu.VMEM)


def smem():
    return pl.BlockSpec(memory_space=pltpu.SMEM)


def hbm():
    return pl.BlockSpec(memory_space=pl.ANY)


def far(array):
    return pltpu.with_memory_space_constraint(array, pltpu.HBM)


def near(array):
    return pltpu.with_memory_space_constraint(array, pltpu.VMEM)


def dot_nt(a, b):
    return lax.dot_general(a, b, (((1,), (1,)), ((), ())), preferred_element_type=F32)


def dot_nn(a, b):
    return jnp.dot(a, b, preferred_element_type=F32)


def iota(shape, dim):
    return lax.broadcasted_iota(jnp.int32, shape, dim)


class Stream:
    def __init__(self, groups, ahead):
        self.groups = groups
        self.started = 0
        self.done = 0
        self.start_up_to(ahead)

    def start_up_to(self, count):
        while self.started < min(count, len(self.groups)):
            for copy in self.groups[self.started]:
                copy.start()
            self.started += 1

    def need(self, count):
        while self.done < count:
            for copy in self.groups[self.done]:
                copy.wait()
            self.done += 1
            self.start_up_to(self.started + 1)


def norm_kernel(hidden_hbm, gain_hbm, out_ref, hidden_ref, gain_ref, rows_ref, sem):
    copies = [
        pltpu.make_async_copy(hidden_hbm, hidden_ref, sem.at[0]),
        pltpu.make_async_copy(gain_hbm, gain_ref, sem.at[1]),
    ]
    for copy in copies:
        copy.start()
    local, steps, _ = hidden_ref.shape
    rows_ref[...] = jnp.zeros_like(rows_ref)
    for copy in copies:
        copy.wait()
    for j in range(local):
        rows_ref[pl.ds(j * steps, steps), :] = hidden_ref[j]
    rows = rows_ref[...]
    mean_square = jnp.mean(rows * rows, axis=-1, keepdims=True)
    out_ref[...] = (rows * lax.rsqrt(mean_square + 1e-06) * gain_ref[...]).astype(BF16)


def norm_rows(hidden, gain):
    width = hidden.shape[2]
    return pl.pallas_call(
        norm_kernel,
        out_shape=jax.ShapeDtypeStruct((GROUP, width), BF16),
        in_specs=[hbm(), hbm()],
        out_specs=vmem(),
        scratch_shapes=[
            pltpu.VMEM(hidden.shape, F32),
            pltpu.VMEM((1, width), F32),
            pltpu.VMEM((GROUP, width), F32),
            pltpu.SemaphoreType.DMA((2,)),
        ],
        compiler_params=pltpu.CompilerParams(vmem_limit_bytes=4 * MIB),
        name="norm_rows",
    )(far(hidden), far(gain.reshape(1, width)))


def rotated(full, cosine, sine):
    heads = full.shape[1] // HD
    parts = []
    for h in range(heads):
        one = full[:, h * HD : (h + 1) * HD]
        parts.append(one * cosine + pltpu.roll(one, HD // 2, 1) * sine)
    return jnp.concatenate(parts, axis=1)


def rotation(lens_ref, groups, local, steps):
    group_row = iota((GROUP, HD), 0)
    places = []
    for g in range(groups):
        place = group_row % steps
        for j in range(local):
            here = group_row // steps == j
            place = place + jnp.where(here, lens_ref[g * local + j], 0)
        places.append(place)
    half = HD // 2
    lane = iota((1, HD), 1) % half
    frequency = jnp.zeros((1, HD), F32)
    for i in range(half):
        frequency = jnp.where(lane == i, float(np.float32(10000.0 ** (-i / half))), frequency)
    angles = jnp.concatenate(places, axis=0).astype(F32) * frequency
    sine = jnp.sin(angles)
    return jnp.cos(angles), jnp.where(iota(sine.shape, 1) < half, -sine, sine)


def spread_heads(queries, requests, local, steps):
    per = queries.shape[1] // HD * steps
    picked = iota((requests * per, queries.shape[0]), 0)
    request, inside = picked // per, picked % per
    source = request // local * GROUP + request % local * steps + inside % steps
    choose = (source == iota(picked.shape, 1)).astype(BF16)
    wide = dot_nn(choose, queries)
    head_of = iota(wide.shape, 0) % per // steps
    return jnp.where(head_of == iota(wide.shape, 1) // HD, wide, 0.0).astype(BF16)


def own_head(mixed, steps):
    rows, width = mixed.shape
    heads = width // HD
    head = iota((rows, HD), 0) % (heads * steps) // steps
    result = mixed[:, :HD]
    for h in range(1, heads):
        result = jnp.where(head == h, mixed[:, h * HD : (h + 1) * HD], result)
    return result


def slot_place(lens_ref, slot_req_ref, slot_block_ref, s, block):
    wanted = slot_req_ref[s]
    request = jnp.maximum(wanted, 0)
    base = lens_ref[request] - slot_block_ref[s] * block
    return request, jnp.where(wanted >= 0, base, -4 * block)


def patch_slots(slot_facts, local, steps, buf, new, low, high):
    _, block, width = buf.shape
    patch_rows = iota((16, width), 0)

    def one(s, carry):
        request, base = slot_facts(s)

        @pl.when((base > -steps) & (base < block))
        def _():
            first = request // local * GROUP + request % local * steps
            for t in range(steps):
                row = base + t

                @pl.when((row >= 0) & (row < block))
                def _():
                    start = pl.multiple_of(row // 16 * 16, 16)
                    hit = patch_rows == row - start
                    old = buf[s, pl.ds(start, 16), :].astype(F32)
                    fresh = new[pl.ds(first + t, 1), :]
                    buf[s, pl.ds(start, 16), :] = jnp.where(hit, fresh, old).astype(BF16)

        return carry

    lax.fori_loop(low, high, one, 0)


def attention_kernel(
    local,
    steps,
    lens_hbm,
    slot_req_hbm,
    slot_block_hbm,
    rows_ref,
    query_hbm,
    key_in,
    value_in,
    part_ref,
    queries_ref,
    weight,
    key_buf,
    value_buf,
    spread,
    scores_buf,
    weight_buf,
    slot_max,
    slot_total,
    slot_out,
    req_max,
    req_total,
    req_out,
    lens_ref,
    slot_req_ref,
    slot_block_ref,
    weight_sem,
    in_sem,
    small_sem,
):
    pool, block, width = key_buf.shape
    heads = width // HD
    per = heads * steps
    requests = req_max.shape[0]
    groups = requests // local
    chunks = [(c, min(c + CHUNK, pool)) for c in range(0, pool, CHUNK)]

    weight_copy = pltpu.make_async_copy(query_hbm, weight, weight_sem.at[0])

    def moves(source, target, sems, n):
        return [
            pltpu.make_async_copy(
                source.at[pl.ds(low, high - low)], target.at[pl.ds(low, high - low)], sems.at[n, i]
            )
            for i, (low, high) in enumerate(chunks)
        ]

    keys_in = moves(key_in, key_buf, in_sem, 0)
    values_in = moves(value_in, value_buf, in_sem, 1)
    small_copies = [
        pltpu.make_async_copy(source, target, small_sem.at[i])
        for i, (source, target) in enumerate(
            (
                (lens_hbm, lens_ref),
                (slot_req_hbm, slot_req_ref),
                (slot_block_hbm, slot_block_ref),
            )
        )
    ]
    for copy in small_copies:
        copy.start()
    stream = Stream([[copy] for copy in [weight_copy] + keys_in + values_in], AHEAD)
    for copy in small_copies:
        copy.wait()

    cosine, sine = rotation(lens_ref, groups, local, steps)
    stream.need(1)
    queries = rotated(dot_nn(rows_ref[...], weight[...]), cosine, sine).astype(BF16)
    queries_ref[...] = queries
    spread[...] = spread_heads(queries, requests, local, steps).reshape(requests, per, width)

    def slot_facts(s):
        return slot_place(lens_ref, slot_req_ref, slot_block_ref, s, block)

    def pairs(low, high):
        return [(s, min(s + 2, high)) for s in range(low, high, 2)]

    for i, (low, high) in enumerate(chunks):
        stream.need(2 + i)
        for a, b in pairs(low, high):
            left = jnp.concatenate([spread[slot_facts(s)[0]] for s in range(a, b)], axis=0)
            right = key_buf[pl.ds(a, b - a)].reshape((b - a) * block, width)
            both = dot_nt(left, right)
            for s in range(a, b):
                n = s - a
                scores_buf[s] = both[n * per : (n + 1) * per, n * block : (n + 1) * block]

    scale = 1.0 / math.sqrt(HD)
    position = iota((per, block), 1)
    for s in range(pool):
        allowed = position < slot_facts(s)[1]
        scores = jnp.where(allowed, scores_buf[s] * scale, NEG)
        top = jnp.max(scores, axis=-1, keepdims=True)
        weight = jnp.where(allowed, jnp.exp(scores - top), 0.0)
        slot_max[s] = jnp.broadcast_to(top, (per, HD))
        slot_total[s] = jnp.broadcast_to(jnp.sum(weight, axis=-1, keepdims=True), (per, HD))
        weight_buf[s] = weight.astype(BF16)

    req_max[...] = jnp.full_like(req_max, NEG)
    for s in range(pool):
        request = slot_facts(s)[0]
        req_max[request] = jnp.maximum(req_max[request], slot_max[s])

    for i, (low, high) in enumerate(chunks):
        stream.need(2 + len(chunks) + i)
        for a, b in pairs(low, high):
            pieces = []
            for s in range(a, b):
                row = [jnp.zeros((per, block), BF16)] * (b - a)
                row[s - a] = weight_buf[s]
                pieces.append(jnp.concatenate(row, axis=1))
            left = jnp.concatenate(pieces, axis=0)
            mixed = dot_nn(left, value_buf[pl.ds(a, b - a)].reshape((b - a) * block, width))
            for s in range(a, b):
                slot_out[s] = own_head(mixed[(s - a) * per : (s - a + 1) * per], steps)

    for s in range(pool):
        factor = jnp.exp(slot_max[s] - req_max[slot_facts(s)[0]])
        slot_total[s] = factor * slot_total[s]
        slot_out[s] = factor * slot_out[s]
    req_total[...] = jnp.zeros_like(req_total)
    req_out[...] = jnp.zeros_like(req_out)
    for s in range(pool):
        request = slot_facts(s)[0]
        req_total[request] = req_total[request] + slot_total[s]
        req_out[request] = req_out[request] + slot_out[s]

    total = req_total[...]
    some = total > 0.0
    safe = jnp.where(some, total, 1.0)
    mean = jnp.where(some, req_out[...] / safe, 0.0).astype(BF16)
    level = jnp.where(some, req_max[...] + jnp.log(safe), NEG)
    high = level.astype(BF16).astype(F32)
    middle = (level - high).astype(BF16).astype(F32)
    low_part = (level - high - middle).astype(BF16).astype(F32)
    row = iota(level.shape, 1)
    lane = iota(level.shape, 2)
    packed = jnp.where(lane == row, high, 0.0)
    packed = packed + jnp.where(lane == row + per, middle, 0.0)
    packed = packed + jnp.where(lane == row + 2 * per, low_part, 0.0)
    packed = jnp.sum(packed, axis=1, keepdims=True)
    block_row = iota((16, HD), 0)
    for g in range(groups):
        levels = jnp.zeros((16, HD), F32)
        for j in range(local):
            b = g * local + j
            part_ref[g, pl.ds(j * per, per), :] = mean[b]
            levels = jnp.where(block_row == j, packed[b], levels)
        part_ref[g, pl.ds(local * per, 16), :] = levels.astype(BF16)


def attention(rows, weight, caches, lens, slot_req, slot_block, local, steps):
    pool, block, width = caches[0].shape
    model = rows.shape[1]
    requests = lens.shape[0]
    per = width // HD * steps
    chunk_count = -(-pool // CHUNK)
    new_shape = jax.ShapeDtypeStruct((rows.shape[0], width), BF16)
    slot_stat = pltpu.VMEM((pool, per, HD), F32)
    req_stat = pltpu.VMEM((requests, per, HD), F32)
    return pl.pallas_call(
        functools.partial(attention_kernel, local, steps),
        out_shape=(
            jax.ShapeDtypeStruct((requests // local, local * per + 16, HD), BF16),
            new_shape,
        ),
        in_specs=[hbm()] * 3 + [vmem()] + [hbm()] * 3,
        out_specs=(vmem(), vmem()),
        scratch_shapes=[
            pltpu.VMEM((model, width), BF16),
            pltpu.VMEM((pool, block, width), BF16),
            pltpu.VMEM((pool, block, width), BF16),
            pltpu.VMEM((requests, per, width), BF16),
            pltpu.VMEM((pool, per, block), F32),
            pltpu.VMEM((pool, per, block), BF16),
            slot_stat,
            slot_stat,
            slot_stat,
            req_stat,
            req_stat,
            req_stat,
            pltpu.SMEM(lens.shape, jnp.int32),
            pltpu.SMEM(slot_req.shape, jnp.int32),
            pltpu.SMEM(slot_block.shape, jnp.int32),
            pltpu.SemaphoreType.DMA((1,)),
            pltpu.SemaphoreType.DMA((2, chunk_count)),
            pltpu.SemaphoreType.DMA((3,)),
        ],
        compiler_params=pltpu.CompilerParams(vmem_limit_bytes=28 * MIB),
        name="attention",
    )(
        far(lens),
        far(slot_req),
        far(slot_block),
        rows,
        far(weight),
        *[far(array) for array in caches],
    )


def fresh_kernel(
    local,
    steps,
    lens_ref,
    rows_ref,
    queries_ref,
    key_hbm,
    value_hbm,
    keys_ref,
    values_ref,
    mean_ref,
    level_ref,
    weights,
    sem,
):
    copies = [
        pltpu.make_async_copy(source, weights.at[n], sem.at[n])
        for n, source in enumerate((key_hbm, value_hbm))
    ]
    for copy in copies:
        copy.start()
    groups = rows_ref.shape[0] // GROUP
    width = keys_ref.shape[1]
    per = width // HD * steps
    own = pl.ds(pl.multiple_of(lax.axis_index("seq") * GROUP, GROUP), GROUP)
    spread = spread_heads(queries_ref[own, :], local, local, steps)
    cosine, sine = rotation(lens_ref, groups, local, steps)
    rows = rows_ref[...]
    for copy in copies:
        copy.wait()
    keys_ref[...] = rotated(dot_nn(rows, weights[0]), cosine, sine).astype(BF16)
    values_ref[...] = dot_nn(rows, weights[1]).astype(BF16)
    scores = dot_nt(spread, keys_ref[own, :]) * (1.0 / math.sqrt(HD))
    row = iota(scores.shape, 0)
    column = iota(scores.shape, 1)
    allowed = (column // steps == row // per) & (column % steps <= row % steps)
    scores = jnp.where(allowed, scores, NEG)
    top = jnp.max(scores, axis=-1, keepdims=True)
    weight = jnp.where(allowed, jnp.exp(scores - top), 0.0)
    total = jnp.sum(weight, axis=-1, keepdims=True)
    mixed = own_head(dot_nn(weight.astype(BF16), values_ref[own, :]), steps)
    mean_ref[...] = mixed / total
    level_ref[...] = jnp.broadcast_to(top + jnp.log(total), level_ref.shape)


def fresh_rows(rows, queries, weights, lens, local, steps):
    model, width = weights[0].shape
    count = local * (width // HD) * steps
    new_shape = jax.ShapeDtypeStruct((rows.shape[0], width), BF16)
    own_shape = jax.ShapeDtypeStruct((count, HD), F32)
    return pl.pallas_call(
        functools.partial(fresh_kernel, local, steps),
        out_shape=(new_shape, new_shape, own_shape, own_shape),
        in_specs=[smem()] + [vmem()] * 2 + [hbm()] * 2,
        out_specs=(vmem(),) * 4,
        scratch_shapes=[pltpu.VMEM((2, model, width), BF16), pltpu.SemaphoreType.DMA((2,))],
        compiler_params=pltpu.CompilerParams(vmem_limit_bytes=12 * MIB),
        cost_estimate=pl.CostEstimate(
            flops=4 * rows.shape[0] * model * width,
            bytes_accessed=4 * model * width,
            transcendentals=0,
        ),
        name="fresh_rows",
    )(far(lens), rows, queries, *[far(array) for array in weights])


def cache_kernel(
    local,
    steps,
    lens_ref,
    slot_req_ref,
    slot_block_ref,
    keys_ref,
    values_ref,
    _,
    key_in,
    value_in,
    key_out,
    value_out,
    new_keys,
    new_values,
    key_buf,
    value_buf,
    in_sem,
    out_sem,
):
    pool, block, _ = key_in.shape
    cuts = [(low, min(low + CHUNK, pool)) for low in range(0, pool, CHUNK)]
    caches = ((key_in, key_buf, key_out, new_keys), (value_in, value_buf, value_out, new_values))
    steps_of = [(n, i) for n in range(2) for i in range(len(cuts))]

    def move(source, target, sem, n, i):
        low, high = cuts[i]
        span = pl.ds(low, high - low)
        return pltpu.make_async_copy(source.at[span], target.at[span], sem.at[n, i])

    stream = Stream([[move(caches[n][0], caches[n][1], in_sem, n, i)] for n, i in steps_of], AHEAD)
    outs = [move(caches[n][1], caches[n][2], out_sem, n, i) for n, i in steps_of]
    new_keys[...] = keys_ref[...].astype(F32)
    new_values[...] = values_ref[...].astype(F32)

    def slot_facts(s):
        return slot_place(lens_ref, slot_req_ref, slot_block_ref, s, block)

    for k, (n, i) in enumerate(steps_of):
        stream.need(k + 1)
        patch_slots(slot_facts, local, steps, caches[n][1], caches[n][3], *cuts[i])
        outs[k].start()
    for copy in outs:
        copy.wait()


def updated_caches(caches, keys, values, lens, slot_req, slot_block, after, local, steps):
    pool, block, width = caches[0].shape
    cache_shape = jax.ShapeDtypeStruct(caches[0].shape, BF16)
    return pl.pallas_call(
        functools.partial(cache_kernel, local, steps),
        out_shape=(cache_shape, cache_shape),
        in_specs=[smem()] * 3 + [vmem()] * 2 + [hbm()] * 3,
        out_specs=(hbm(), hbm()),
        scratch_shapes=[pltpu.VMEM(keys.shape, F32)] * 2
        + [pltpu.VMEM((pool, block, width), BF16)] * 2
        + [pltpu.SemaphoreType.DMA((2, -(-pool // CHUNK)))] * 2,
        compiler_params=pltpu.CompilerParams(vmem_limit_bytes=20 * MIB),
        cost_estimate=pl.CostEstimate(
            flops=0, bytes_accessed=4 * 2 * pool * block * width, transcendentals=0
        ),
        name="updated_caches",
    )(far(lens), far(slot_req), far(slot_block), keys, values, after, *[far(array) for array in caches])


def merge_kernel(local, steps, part_ref, mean_ref, level_ref, weight_ref, out_ref):
    holders = part_ref.shape[0]
    width = weight_ref.shape[0]
    heads = width // HD
    per = heads * steps
    count = local * per
    values = [part_ref[g, pl.ds(0, count), :].astype(F32) for g in range(holders)]
    row = iota((count, HD), 0)
    lane = iota((count, HD), 1)
    mine = (lane % per == row % per) & (lane < 3 * per)
    levels = []
    for g in range(holders):
        stat = part_ref[g, pl.ds(count, 16), :].astype(F32)
        wide = jnp.concatenate(
            [jnp.broadcast_to(stat[j : j + 1], (per, HD)) for j in range(local)], axis=0
        )
        levels.append(jnp.sum(jnp.where(mine, wide, 0.0), axis=-1, keepdims=True))
    values.append(mean_ref[...])
    levels.append(level_ref[:, :1])
    top = functools.reduce(jnp.maximum, levels)
    shares = [jnp.exp(level - top) for level in levels]
    total = sum(shares)
    mixed = sum(share * value for share, value in zip(shares, values))
    attended = (mixed / total).astype(BF16)
    target = iota((GROUP, count), 0)
    source = iota((GROUP, count), 1)
    parts = []
    for h in range(heads):
        pick = (source == target // steps * per + h * steps + target % steps) & (
            target < local * steps
        )
        parts.append(dot_nn(pick.astype(BF16), attended).astype(BF16))
    out_ref[...] = dot_nn(jnp.concatenate(parts, axis=1), weight_ref[...]).astype(BF16)


def merge_project(parts, mean, level, out_weight, local, steps):
    return pl.pallas_call(
        functools.partial(merge_kernel, local, steps),
        out_shape=jax.ShapeDtypeStruct((GROUP, out_weight.shape[1]), BF16),
        in_specs=[vmem()] * 4,
        out_specs=vmem(),
        compiler_params=pltpu.CompilerParams(vmem_limit_bytes=8 * MIB),
        name="merge_project",
    )(parts, mean, level, out_weight)


def second_norm_kernel(hidden_ref, left_ref, right_ref, gain_ref, ids_ref, gates_ref, rows_out, res_out, rows_ref):
    local, steps, width = hidden_ref.shape
    rows_ref[...] = jnp.zeros_like(rows_ref)
    for j in range(local):
        rows_ref[pl.ds(j * steps, steps), :] = hidden_ref[j]
    residual = rows_ref[...] + (left_ref[...].astype(F32) + right_ref[...].astype(F32))
    res_out[...] = residual
    mean_square = jnp.mean(residual * residual, axis=-1, keepdims=True)
    normed = residual * lax.rsqrt(mean_square + 1e-06) * gain_ref[...]
    rows_out[:, pl.ds(0, width)] = normed.astype(BF16)
    rows_ref[:, pl.ds(0, HD)] = jnp.zeros((GROUP, HD), F32)
    lane = iota((steps, HD), 1)
    for j in range(local):
        table = jnp.zeros((steps, HD), F32)
        for k in range(ids_ref.shape[2]):
            hit = lane % EXPERTS == ids_ref[j, :, k : k + 1]
            table = table + jnp.where(hit, gates_ref[j, :, k : k + 1], 0.0)
        rows_ref[pl.ds(j * steps, steps), pl.ds(0, HD)] = table
    table = rows_ref[:, pl.ds(0, HD)]
    high = table.astype(BF16)
    low = (table - high.astype(F32)).astype(BF16)
    rows_out[:, pl.ds(width, HD)] = jnp.where(iota((GROUP, HD), 1) < EXPERTS, high.astype(F32), low.astype(F32)).astype(BF16)


def second_norm(hidden, left, right, gain, ids, gates):
    width = hidden.shape[2]
    return pl.pallas_call(
        second_norm_kernel,
        out_shape=(
            jax.ShapeDtypeStruct((GROUP, width + HD), BF16),
            jax.ShapeDtypeStruct((GROUP, width), F32),
        ),
        in_specs=[vmem()] * 6,
        out_specs=(vmem(), vmem()),
        scratch_shapes=[pltpu.VMEM((GROUP, width), F32)],
        compiler_params=pltpu.CompilerParams(vmem_limit_bytes=4 * MIB),
        name="second_norm",
    )(hidden, left, right, gain.reshape(1, width), ids, gates)


def shared_window(total, ranks):
    each = total // ranks
    length = max(-(-(r * each % 16 + each) // 16) * 16 for r in range(ranks))
    return each, length


def expert_blocks(hidden, every):
    blocks = [(low, min(low + BLOCK, every)) for low in range(0, every, BLOCK)]
    return blocks, min(FETCHED, sum(high <= hidden for _, high in blocks))


def fetch_kernel(low, rows, _, gate_hbm, up_hbm, gate_ref, up_ref, sem):
    copies = [
        pltpu.make_async_copy(source.at[pl.ds(low, rows)], target, sem.at[n])
        for n, (source, target) in enumerate(((gate_hbm, gate_ref), (up_hbm, up_ref)))
    ]
    for copy in copies:
        copy.start()
    for copy in copies:
        copy.wait()


def fetch(block, gate, up, after):
    low, high = block
    shape = pltpu.VMEM((high - low, gate.shape[1]), BF16)
    return pl.pallas_call(
        functools.partial(fetch_kernel, low, high - low),
        out_shape=(shape, shape),
        in_specs=[hbm()] * 3,
        out_specs=(vmem(), vmem()),
        scratch_shapes=[pltpu.SemaphoreType.DMA((2,))],
        compiler_params=pltpu.CompilerParams(vmem_limit_bytes=MIB),
        cost_estimate=pl.CostEstimate(
            flops=0, bytes_accessed=4 * (high - low) * gate.shape[1], transcendentals=0
        ),
        name="fetch_weights",
    )(after, far(gate), far(up))


def packs(tokens, columns):
    return tokens == 12 and columns == 4 * HD


def experts_kernel(
    tokens,
    count,
    ranks,
    fetched,
    rows_ref,
    *refs,
):
    early = [(refs[2 * i], refs[2 * i + 1]) for i in range(fetched)]
    streamed_experts(tokens, count, ranks, early, rows_ref, *refs[2 * fetched :])


def streamed_experts(
    tokens,
    count,
    ranks,
    early,
    rows_ref,
    gate_hbm,
    up_hbm,
    down_hbm,
    shared_gate_hbm,
    shared_up_hbm,
    shared_down_hbm,
    out_ref,
    gate_ref,
    up_ref,
    down_ref,
    inner_ref,
    total_ref,
    sem,
    shared_sem,
):
    hidden, width = gate_hbm.shape
    every = down_ref.shape[0]
    each = hidden // count
    slim, length = shared_window(shared_gate_hbm.shape[0], ranks)
    seq_rank = lax.axis_index("seq")
    slim_low = seq_rank * slim
    slim_start = pl.multiple_of(
        jnp.minimum(slim_low // 16 * 16, shared_gate_hbm.shape[0] - length), 16
    )
    blocks, _ = expert_blocks(hidden, every)
    skipped = blocks[len(early) - 1][1] if early else 0

    def moves(source, extra, target, n, skip):
        copies = []
        for i, (low, high) in enumerate(blocks):
            top = min(high, hidden)
            piece = []
            if low < skip:
                continue
            if top > low:
                piece.append(
                    pltpu.make_async_copy(
                        source.at[pl.ds(low, top - low)],
                        target.at[pl.ds(low - skip, top - low)],
                        sem.at[n, i],
                    )
                )
            if high == every:
                piece.append(
                    pltpu.make_async_copy(
                        extra.at[pl.ds(slim_start, length)],
                        target.at[pl.ds(hidden - skip, length)],
                        shared_sem.at[n],
                    )
                )
            copies.append(piece)
        return copies

    gates = moves(gate_hbm, shared_gate_hbm, gate_ref, 0, skipped)
    ups = moves(up_hbm, shared_up_hbm, up_ref, 1, skipped)
    downs = moves(down_hbm, shared_down_hbm, down_ref, 2, 0)
    stream = Stream([a + b for a, b in zip(gates, ups)] + downs, 2)

    first = seq_rank * count
    rows = rows_ref[:, pl.ds(0, width)]
    table = rows_ref[:, pl.ds(width, HD)]
    for i, (low, high) in enumerate(blocks):
        shape = (HD, high - low)
        unit = low + iota(shape, 1)
        expert = jnp.where(unit < hidden, first + unit // each, -1)
        share = dot_nn(table, (iota(shape, 0) % EXPERTS == expert).astype(BF16))
        if high > hidden:
            unit = low + iota(share.shape, 1) - hidden + slim_start
            mine = (unit >= slim_low) & (unit < slim_low + slim)
            in_shared = low + iota(share.shape, 1) >= hidden
            share = jnp.where(in_shared, mine.astype(F32), share)
        if i < len(early):
            gate_block, up_block = (ref[...] for ref in early[i])
        else:
            stream.need(i + 1 - len(early))
            gate_block = gate_ref[pl.ds(low - skipped, high - low), :]
            up_block = up_ref[pl.ds(low - skipped, high - low), :]
        gate = dot_nt(rows, gate_block)
        up = dot_nt(rows, up_block)
        inner_ref[:, pl.ds(low, high - low)] = (jax.nn.silu(gate) * up * share).astype(BF16)

    groups = total_ref.shape[0] // GROUP
    pieces = out_ref.shape[0] // groups
    columns = width // pieces
    for i, (low, high) in enumerate(blocks):
        stream.need(len(gates) + 1 + i)
        part = inner_ref[:, pl.ds(low, high - low)]
        for p in range(pieces):
            cut = pl.ds(p * columns, columns)
            sums = dot_nn(part, down_ref[pl.ds(low, high - low), cut])
            if i > 0:
                sums = sums + total_ref[:, cut]
            if i < len(blocks) - 1:
                total_ref[:, cut] = sums
            elif packs(tokens, columns):
                last = sums[:, 3 * HD :]
                body_row = iota(last.shape, 0) % GROUP < tokens
                for c in range(3):
                    moved = pltpu.roll(last, tokens - 4 * c, 0)
                    tile = jnp.where(body_row, sums[:, c * HD : (c + 1) * HD], moved).astype(BF16)
                    for g in range(groups):
                        out_ref[g * pieces + p, pl.ds(c * GROUP, GROUP), :] = tile[
                            g * GROUP : (g + 1) * GROUP
                        ]
            else:
                for g in range(groups):
                    out_ref[g * pieces + p] = sums[g * GROUP : g * GROUP + tokens].astype(BF16)


def all_experts(rows, early, routed, shared, tokens, pieces):
    count, each, width = routed[2].shape
    hidden = count * each
    groups = rows.shape[0] // GROUP
    every = hidden + shared_window(shared[2].shape[0], groups)[1]
    routed = [array.reshape(hidden, width) for array in routed]
    early = [array for pair in early for array in pair]
    shape = (tokens, width // pieces)
    if packs(*shape):
        shape = (3 * GROUP, HD)
    rest = every - sum(array.shape[0] for array in early) // 2
    return pl.pallas_call(
        functools.partial(experts_kernel, tokens, count, groups, len(early) // 2),
        out_shape=jax.ShapeDtypeStruct((groups * pieces, *shape), BF16),
        in_specs=[vmem()] * (1 + len(early)) + [hbm()] * 6,
        out_specs=vmem(),
        scratch_shapes=[pltpu.VMEM((rest, width), BF16)] * 2
        + [
            pltpu.VMEM((every, width), BF16),
            pltpu.VMEM((rows.shape[0], every), BF16),
            pltpu.VMEM((rows.shape[0], width), F32),
            pltpu.SemaphoreType.DMA((3, -(-every // BLOCK))),
            pltpu.SemaphoreType.DMA((3,)),
        ],
        compiler_params=pltpu.CompilerParams(
            vmem_limit_bytes=(2 * rest + every) * width * 2 + 8 * MIB
        ),
        name="experts",
    )(rows, *[near(array) for array in early], *[far(array) for array in (*routed, *shared)])


def last_kernel(res_ref, parts_ref, out_ref):
    local, steps, columns = out_ref.shape
    total = parts_ref[0].astype(F32)
    for i in range(1, parts_ref.shape[0]):
        total = total + parts_ref[i].astype(F32)
    cut = pl.ds(pl.multiple_of(lax.axis_index("exp") * columns, HD), columns)
    for j in range(local):
        rows = slice(j * steps, (j + 1) * steps)
        own = res_ref[pl.ds(j * steps, steps), cut]
        if packs(local * steps, columns):
            for c in range(4):
                start = c * GROUP + j * steps if c < 3 else j * GROUP + local * steps
                lanes = slice(c * HD, (c + 1) * HD)
                out_ref[j, :, lanes] = own[:, lanes] + total[start : start + steps]
        else:
            out_ref[j] = own + total[rows]


def last_sum(residual, parts, local, steps, columns):
    return pl.pallas_call(
        last_kernel,
        out_shape=jax.ShapeDtypeStruct((local, steps, columns), F32),
        in_specs=[vmem(), vmem()],
        out_specs=vmem(),
        compiler_params=pltpu.CompilerParams(vmem_limit_bytes=8 * MIB),
        name="last_sum",
    )(residual, parts)


def partner(array, axis, bit):
    count = lax.axis_size(axis)
    return lax.ppermute(array, axis, [(i, i ^ bit) for i in range(count)])


def body(
    hidden_in,
    cache_lens,
    slot_request,
    slot_block,
    key_cache,
    value_cache,
    attn_gain,
    query_weight,
    key_weight,
    value_weight,
    out_weight,
    ffn_gain,
    expert_ids,
    expert_weights,
    gate_experts,
    up_experts,
    down_experts,
    gate_shared,
    up_shared,
    down_shared,
):
    local, steps, width = hidden_in.shape
    exp_count = lax.axis_size("exp")
    tokens = local * steps

    normed = norm_rows(hidden_in, attn_gain)
    rows = lax.all_gather(normed, "seq", axis=0, tiled=True)
    parts, queries = attention(
        rows,
        query_weight,
        (key_cache, value_cache),
        cache_lens,
        slot_request,
        slot_block,
        local,
        steps,
    )
    parts = lax.all_to_all(parts, "seq", split_axis=0, concat_axis=0, tiled=True)
    new_keys, new_values, mean, level = fresh_rows(
        rows, queries, (key_weight, value_weight), cache_lens, local, steps
    )
    terms = merge_project(parts, mean, level, out_weight, local, steps)
    gate_rows = jnp.swapaxes(gate_experts, 1, 2).reshape(-1, width)
    up_rows = jnp.swapaxes(up_experts, 1, 2).reshape(-1, width)
    hidden = gate_rows.shape[0]
    extra = shared_window(down_shared.shape[0], lax.axis_size("seq"))[1]
    blocks, fetched = expert_blocks(hidden, hidden + extra)
    early = []
    other = partner(terms, "exp", 1)
    bit = 2
    while bit < exp_count:
        if len(early) < fetched:
            early.append(fetch(blocks[len(early)], gate_rows, up_rows, terms))
            other, early[-1] = lax.optimization_barrier((other, early[-1]))
        terms = (terms.astype(F32) + other.astype(F32)).astype(BF16)
        other = partner(terms, "exp", bit)
        bit *= 2
    while len(early) < fetched:
        early.append(fetch(blocks[len(early)], gate_rows, up_rows, terms))
    ffn_in, residual = second_norm(
        hidden_in, terms, other, ffn_gain, expert_ids, expert_weights
    )
    all_rows = lax.all_gather(ffn_in, "seq", axis=0, tiled=True)
    sums = all_experts(
        all_rows,
        early,
        (jnp.swapaxes(gate_experts, 1, 2), jnp.swapaxes(up_experts, 1, 2), down_experts),
        (jnp.swapaxes(gate_shared, 0, 1), jnp.swapaxes(up_shared, 0, 1), down_shared),
        tokens,
        exp_count,
    )
    key_out, value_out = updated_caches(
        (key_cache, value_cache),
        new_keys,
        new_values,
        cache_lens,
        slot_request,
        slot_block,
        sums,
        local,
        steps,
    )
    sums = lax.all_to_all(sums, ("seq", "exp"), split_axis=0, concat_axis=0, tiled=True)
    hidden_out = last_sum(residual, sums, local, steps, width // exp_count)
    return hidden_out, key_out, value_out


def solution(mesh):
    in_specs = (
        P("seq", None, None),
        P(),
        P("seq"),
        P("seq"),
        P("seq", None, "exp"),
        P("seq", None, "exp"),
        P(),
        P(None, "exp"),
        P(None, "exp"),
        P(None, "exp"),
        P("exp", None),
        P(),
        P("seq", None, None),
        P("seq", None, None),
        P("seq", None, "exp"),
        P("seq", None, "exp"),
        P("seq", "exp", None),
        P(None, "exp"),
        P(None, "exp"),
        P("exp", None),
    )
    out_specs = (P("seq", None, "exp"), P("seq", None, "exp"), P("seq", None, "exp"))
    return jax.shard_map(body, mesh=mesh, in_specs=in_specs, out_specs=out_specs, check_vma=False)
```

```python
import functools
import math

import jax
import jax.numpy as jnp
import numpy as np
from jax import lax
from jax.experimental import pallas as pl
from jax.experimental.pallas import tpu as pltpu
from jax.sharding import PartitionSpec as P

HD = 128
EXPERTS = 64
GROUP = 16
BLOCK = 768
FETCHED = 2
AHEAD = 2
CHUNK = 46
NEG = -1e30
MIB = 1 << 20
F32 = jnp.float32
BF16 = jnp.bfloat16


def vmem():
    return pl.BlockSpec(memory_space=pltpu.VMEM)


def smem():
    return pl.BlockSpec(memory_space=pltpu.SMEM)


def hbm():
    return pl.BlockSpec(memory_space=pl.ANY)


def far(array):
    return pltpu.with_memory_space_constraint(array, pltpu.HBM)


def near(array):
    return pltpu.with_memory_space_constraint(array, pltpu.VMEM)


def dot_nt(a, b):
    return lax.dot_general(a, b, (((1,), (1,)), ((), ())), preferred_element_type=F32)


def dot_nn(a, b):
    return jnp.dot(a, b, preferred_element_type=F32)


def iota(shape, dim):
    return lax.broadcasted_iota(jnp.int32, shape, dim)


class Stream:
    def __init__(self, groups, ahead):
        self.groups = groups
        self.started = 0
        self.done = 0
        self.start_up_to(ahead)

    def start_up_to(self, count):
        while self.started < min(count, len(self.groups)):
            for copy in self.groups[self.started]:
                copy.start()
            self.started += 1

    def need(self, count):
        while self.done < count:
            for copy in self.groups[self.done]:
                copy.wait()
            self.done += 1
            self.start_up_to(self.started + 1)


def norm_kernel(hidden_hbm, gain_hbm, out_ref, hidden_ref, gain_ref, rows_ref, sem):
    copies = [
        pltpu.make_async_copy(hidden_hbm, hidden_ref, sem.at[0]),
        pltpu.make_async_copy(gain_hbm, gain_ref, sem.at[1]),
    ]
    for copy in copies:
        copy.start()
    local, steps, _ = hidden_ref.shape
    rows_ref[...] = jnp.zeros_like(rows_ref)
    for copy in copies:
        copy.wait()
    for j in range(local):
        rows_ref[pl.ds(j * steps, steps), :] = hidden_ref[j]
    rows = rows_ref[...]
    mean_square = jnp.mean(rows * rows, axis=-1, keepdims=True)
    out_ref[...] = (rows * lax.rsqrt(mean_square + 1e-06) * gain_ref[...]).astype(BF16)


def norm_rows(hidden, gain):
    width = hidden.shape[2]
    return pl.pallas_call(
        norm_kernel,
        out_shape=jax.ShapeDtypeStruct((GROUP, width), BF16),
        in_specs=[hbm(), hbm()],
        out_specs=vmem(),
        scratch_shapes=[
            pltpu.VMEM(hidden.shape, F32),
            pltpu.VMEM((1, width), F32),
            pltpu.VMEM((GROUP, width), F32),
            pltpu.SemaphoreType.DMA((2,)),
        ],
        compiler_params=pltpu.CompilerParams(vmem_limit_bytes=4 * MIB),
        name="norm_rows",
    )(far(hidden), far(gain.reshape(1, width)))


def rotated(full, cosine, sine):
    heads = full.shape[1] // HD
    parts = []
    for h in range(heads):
        one = full[:, h * HD : (h + 1) * HD]
        parts.append(one * cosine + pltpu.roll(one, HD // 2, 1) * sine)
    return jnp.concatenate(parts, axis=1)


def rotation(lens_ref, groups, local, steps):
    group_row = iota((GROUP, HD), 0)
    places = []
    for g in range(groups):
        place = group_row % steps
        for j in range(local):
            here = group_row // steps == j
            place = place + jnp.where(here, lens_ref[g * local + j], 0)
        places.append(place)
    half = HD // 2
    lane = iota((1, HD), 1) % half
    frequency = jnp.zeros((1, HD), F32)
    for i in range(half):
        frequency = jnp.where(lane == i, float(np.float32(10000.0 ** (-i / half))), frequency)
    angles = jnp.concatenate(places, axis=0).astype(F32) * frequency
    sine = jnp.sin(angles)
    return jnp.cos(angles), jnp.where(iota(sine.shape, 1) < half, -sine, sine)


def spread_heads(queries, requests, local, steps):
    per = queries.shape[1] // HD * steps
    picked = iota((requests * per, queries.shape[0]), 0)
    request, inside = picked // per, picked % per
    source = request // local * GROUP + request % local * steps + inside % steps
    choose = (source == iota(picked.shape, 1)).astype(BF16)
    wide = dot_nn(choose, queries)
    head_of = iota(wide.shape, 0) % per // steps
    return jnp.where(head_of == iota(wide.shape, 1) // HD, wide, 0.0).astype(BF16)


def own_head(mixed, steps):
    rows, width = mixed.shape
    heads = width // HD
    head = iota((rows, HD), 0) % (heads * steps) // steps
    result = mixed[:, :HD]
    for h in range(1, heads):
        result = jnp.where(head == h, mixed[:, h * HD : (h + 1) * HD], result)
    return result


def slot_place(lens_ref, slot_req_ref, slot_block_ref, s, block):
    wanted = slot_req_ref[s]
    request = jnp.maximum(wanted, 0)
    base = lens_ref[request] - slot_block_ref[s] * block
    return request, jnp.where(wanted >= 0, base, -4 * block)


def patch_slots(slot_facts, local, steps, buf, new, low, high):
    _, block, width = buf.shape
    patch_rows = iota((16, width), 0)

    def one(s, carry):
        request, base = slot_facts(s)

        @pl.when((base > -steps) & (base < block))
        def _():
            first = request // local * GROUP + request % local * steps
            for t in range(steps):
                row = base + t

                @pl.when((row >= 0) & (row < block))
                def _():
                    start = pl.multiple_of(row // 16 * 16, 16)
                    hit = patch_rows == row - start
                    old = buf[s, pl.ds(start, 16), :].astype(F32)
                    fresh = new[pl.ds(first + t, 1), :]
                    buf[s, pl.ds(start, 16), :] = jnp.where(hit, fresh, old).astype(BF16)

        return carry

    lax.fori_loop(low, high, one, 0)


def attention_kernel(
    local,
    steps,
    lens_hbm,
    slot_req_hbm,
    slot_block_hbm,
    rows_ref,
    query_hbm,
    key_in,
    value_in,
    part_ref,
    queries_ref,
    weight,
    key_buf,
    value_buf,
    spread,
    scores_buf,
    weight_buf,
    slot_max,
    slot_total,
    slot_out,
    req_max,
    req_total,
    req_out,
    lens_ref,
    slot_req_ref,
    slot_block_ref,
    weight_sem,
    in_sem,
    small_sem,
):
    pool, block, width = key_buf.shape
    heads = width // HD
    per = heads * steps
    requests = req_max.shape[0]
    groups = requests // local
    chunks = [(c, min(c + CHUNK, pool)) for c in range(0, pool, CHUNK)]

    weight_copy = pltpu.make_async_copy(query_hbm, weight, weight_sem.at[0])

    def moves(source, target, sems, n):
        return [
            pltpu.make_async_copy(
                source.at[pl.ds(low, high - low)], target.at[pl.ds(low, high - low)], sems.at[n, i]
            )
            for i, (low, high) in enumerate(chunks)
        ]

    keys_in = moves(key_in, key_buf, in_sem, 0)
    values_in = moves(value_in, value_buf, in_sem, 1)
    small_copies = [
        pltpu.make_async_copy(source, target, small_sem.at[i])
        for i, (source, target) in enumerate(
            (
                (lens_hbm, lens_ref),
                (slot_req_hbm, slot_req_ref),
                (slot_block_hbm, slot_block_ref),
            )
        )
    ]
    for copy in small_copies:
        copy.start()
    stream = Stream([[copy] for copy in [weight_copy] + keys_in + values_in], AHEAD)
    for copy in small_copies:
        copy.wait()

    cosine, sine = rotation(lens_ref, groups, local, steps)
    stream.need(1)
    queries = rotated(dot_nn(rows_ref[...], weight[...]), cosine, sine).astype(BF16)
    queries_ref[...] = queries
    spread[...] = spread_heads(queries, requests, local, steps).reshape(requests, per, width)

    def slot_facts(s):
        return slot_place(lens_ref, slot_req_ref, slot_block_ref, s, block)

    def pairs(low, high):
        return [(s, min(s + 2, high)) for s in range(low, high, 2)]

    for i, (low, high) in enumerate(chunks):
        stream.need(2 + i)
        for a, b in pairs(low, high):
            left = jnp.concatenate([spread[slot_facts(s)[0]] for s in range(a, b)], axis=0)
            right = key_buf[pl.ds(a, b - a)].reshape((b - a) * block, width)
            both = dot_nt(left, right)
            for s in range(a, b):
                n = s - a
                scores_buf[s] = both[n * per : (n + 1) * per, n * block : (n + 1) * block]

    scale = 1.0 / math.sqrt(HD)
    position = iota((per, block), 1)
    for s in range(pool):
        allowed = position < slot_facts(s)[1]
        scores = jnp.where(allowed, scores_buf[s] * scale, NEG)
        top = jnp.max(scores, axis=-1, keepdims=True)
        weight = jnp.where(allowed, jnp.exp(scores - top), 0.0)
        slot_max[s] = jnp.broadcast_to(top, (per, HD))
        slot_total[s] = jnp.broadcast_to(jnp.sum(weight, axis=-1, keepdims=True), (per, HD))
        weight_buf[s] = weight.astype(BF16)

    req_max[...] = jnp.full_like(req_max, NEG)
    for s in range(pool):
        request = slot_facts(s)[0]
        req_max[request] = jnp.maximum(req_max[request], slot_max[s])

    for i, (low, high) in enumerate(chunks):
        stream.need(2 + len(chunks) + i)
        for a, b in pairs(low, high):
            pieces = []
            for s in range(a, b):
                row = [jnp.zeros((per, block), BF16)] * (b - a)
                row[s - a] = weight_buf[s]
                pieces.append(jnp.concatenate(row, axis=1))
            left = jnp.concatenate(pieces, axis=0)
            mixed = dot_nn(left, value_buf[pl.ds(a, b - a)].reshape((b - a) * block, width))
            for s in range(a, b):
                slot_out[s] = own_head(mixed[(s - a) * per : (s - a + 1) * per], steps)

    for s in range(pool):
        factor = jnp.exp(slot_max[s] - req_max[slot_facts(s)[0]])
        slot_total[s] = factor * slot_total[s]
        slot_out[s] = factor * slot_out[s]
    req_total[...] = jnp.zeros_like(req_total)
    req_out[...] = jnp.zeros_like(req_out)
    for s in range(pool):
        request = slot_facts(s)[0]
        req_total[request] = req_total[request] + slot_total[s]
        req_out[request] = req_out[request] + slot_out[s]

    total = req_total[...]
    some = total > 0.0
    safe = jnp.where(some, total, 1.0)
    mean = jnp.where(some, req_out[...] / safe, 0.0).astype(BF16)
    level = jnp.where(some, req_max[...] + jnp.log(safe), NEG)
    high = level.astype(BF16).astype(F32)
    middle = (level - high).astype(BF16).astype(F32)
    low_part = (level - high - middle).astype(BF16).astype(F32)
    row = iota(level.shape, 1)
    lane = iota(level.shape, 2)
    packed = jnp.where(lane == row, high, 0.0)
    packed = packed + jnp.where(lane == row + per, middle, 0.0)
    packed = packed + jnp.where(lane == row + 2 * per, low_part, 0.0)
    packed = jnp.sum(packed, axis=1, keepdims=True)
    block_row = iota((16, HD), 0)
    for g in range(groups):
        levels = jnp.zeros((16, HD), F32)
        for j in range(local):
            b = g * local + j
            part_ref[g, pl.ds(j * per, per), :] = mean[b]
            levels = jnp.where(block_row == j, packed[b], levels)
        part_ref[g, pl.ds(local * per, 16), :] = levels.astype(BF16)


def attention(rows, weight, caches, lens, slot_req, slot_block, local, steps):
    pool, block, width = caches[0].shape
    model = rows.shape[1]
    requests = lens.shape[0]
    per = width // HD * steps
    chunk_count = -(-pool // CHUNK)
    new_shape = jax.ShapeDtypeStruct((rows.shape[0], width), BF16)
    slot_stat = pltpu.VMEM((pool, per, HD), F32)
    req_stat = pltpu.VMEM((requests, per, HD), F32)
    return pl.pallas_call(
        functools.partial(attention_kernel, local, steps),
        out_shape=(
            jax.ShapeDtypeStruct((requests // local, local * per + 16, HD), BF16),
            new_shape,
        ),
        in_specs=[hbm()] * 3 + [vmem()] + [hbm()] * 3,
        out_specs=(vmem(), vmem()),
        scratch_shapes=[
            pltpu.VMEM((model, width), BF16),
            pltpu.VMEM((pool, block, width), BF16),
            pltpu.VMEM((pool, block, width), BF16),
            pltpu.VMEM((requests, per, width), BF16),
            pltpu.VMEM((pool, per, block), F32),
            pltpu.VMEM((pool, per, block), BF16),
            slot_stat,
            slot_stat,
            slot_stat,
            req_stat,
            req_stat,
            req_stat,
            pltpu.SMEM(lens.shape, jnp.int32),
            pltpu.SMEM(slot_req.shape, jnp.int32),
            pltpu.SMEM(slot_block.shape, jnp.int32),
            pltpu.SemaphoreType.DMA((1,)),
            pltpu.SemaphoreType.DMA((2, chunk_count)),
            pltpu.SemaphoreType.DMA((3,)),
        ],
        compiler_params=pltpu.CompilerParams(vmem_limit_bytes=28 * MIB),
        name="attention",
    )(
        far(lens),
        far(slot_req),
        far(slot_block),
        rows,
        far(weight),
        *[far(array) for array in caches],
    )


def fresh_kernel(
    local,
    steps,
    lens_ref,
    rows_ref,
    queries_ref,
    key_hbm,
    value_hbm,
    keys_ref,
    values_ref,
    mean_ref,
    level_ref,
    weights,
    sem,
):
    copies = [
        pltpu.make_async_copy(source, weights.at[n], sem.at[n])
        for n, source in enumerate((key_hbm, value_hbm))
    ]
    for copy in copies:
        copy.start()
    groups = rows_ref.shape[0] // GROUP
    width = keys_ref.shape[1]
    per = width // HD * steps
    own = pl.ds(pl.multiple_of(lax.axis_index("seq") * GROUP, GROUP), GROUP)
    spread = spread_heads(queries_ref[own, :], local, local, steps)
    cosine, sine = rotation(lens_ref, groups, local, steps)
    rows = rows_ref[...]
    for copy in copies:
        copy.wait()
    keys_ref[...] = rotated(dot_nn(rows, weights[0]), cosine, sine).astype(BF16)
    values_ref[...] = dot_nn(rows, weights[1]).astype(BF16)
    scores = dot_nt(spread, keys_ref[own, :]) * (1.0 / math.sqrt(HD))
    row = iota(scores.shape, 0)
    column = iota(scores.shape, 1)
    allowed = (column // steps == row // per) & (column % steps <= row % steps)
    scores = jnp.where(allowed, scores, NEG)
    top = jnp.max(scores, axis=-1, keepdims=True)
    weight = jnp.where(allowed, jnp.exp(scores - top), 0.0)
    total = jnp.sum(weight, axis=-1, keepdims=True)
    mixed = own_head(dot_nn(weight.astype(BF16), values_ref[own, :]), steps)
    mean_ref[...] = mixed / total
    level_ref[...] = jnp.broadcast_to(top + jnp.log(total), level_ref.shape)


def fresh_rows(rows, queries, weights, lens, local, steps):
    model, width = weights[0].shape
    count = local * (width // HD) * steps
    new_shape = jax.ShapeDtypeStruct((rows.shape[0], width), BF16)
    own_shape = jax.ShapeDtypeStruct((count, HD), F32)
    return pl.pallas_call(
        functools.partial(fresh_kernel, local, steps),
        out_shape=(new_shape, new_shape, own_shape, own_shape),
        in_specs=[smem()] + [vmem()] * 2 + [hbm()] * 2,
        out_specs=(vmem(),) * 4,
        scratch_shapes=[pltpu.VMEM((2, model, width), BF16), pltpu.SemaphoreType.DMA((2,))],
        compiler_params=pltpu.CompilerParams(vmem_limit_bytes=12 * MIB),
        cost_estimate=pl.CostEstimate(
            flops=4 * rows.shape[0] * model * width,
            bytes_accessed=4 * model * width,
            transcendentals=0,
        ),
        name="fresh_rows",
    )(far(lens), rows, queries, *[far(array) for array in weights])


def cache_kernel(
    local,
    steps,
    lens_ref,
    slot_req_ref,
    slot_block_ref,
    keys_ref,
    values_ref,
    _,
    key_in,
    value_in,
    key_out,
    value_out,
    new_keys,
    new_values,
    key_buf,
    value_buf,
    in_sem,
    out_sem,
):
    pool, block, _ = key_in.shape
    cuts = [(low, min(low + CHUNK, pool)) for low in range(0, pool, CHUNK)]
    caches = ((key_in, key_buf, key_out, new_keys), (value_in, value_buf, value_out, new_values))
    steps_of = [(n, i) for n in range(2) for i in range(len(cuts))]

    def move(source, target, sem, n, i):
        low, high = cuts[i]
        span = pl.ds(low, high - low)
        return pltpu.make_async_copy(source.at[span], target.at[span], sem.at[n, i])

    stream = Stream([[move(caches[n][0], caches[n][1], in_sem, n, i)] for n, i in steps_of], AHEAD)
    outs = [move(caches[n][1], caches[n][2], out_sem, n, i) for n, i in steps_of]
    new_keys[...] = keys_ref[...].astype(F32)
    new_values[...] = values_ref[...].astype(F32)

    def slot_facts(s):
        return slot_place(lens_ref, slot_req_ref, slot_block_ref, s, block)

    for k, (n, i) in enumerate(steps_of):
        stream.need(k + 1)
        patch_slots(slot_facts, local, steps, caches[n][1], caches[n][3], *cuts[i])
        outs[k].start()
    for copy in outs:
        copy.wait()


def updated_caches(caches, keys, values, lens, slot_req, slot_block, after, local, steps):
    pool, block, width = caches[0].shape
    cache_shape = jax.ShapeDtypeStruct(caches[0].shape, BF16)
    return pl.pallas_call(
        functools.partial(cache_kernel, local, steps),
        out_shape=(cache_shape, cache_shape),
        in_specs=[smem()] * 3 + [vmem()] * 2 + [hbm()] * 3,
        out_specs=(hbm(), hbm()),
        scratch_shapes=[pltpu.VMEM(keys.shape, F32)] * 2
        + [pltpu.VMEM((pool, block, width), BF16)] * 2
        + [pltpu.SemaphoreType.DMA((2, -(-pool // CHUNK)))] * 2,
        compiler_params=pltpu.CompilerParams(vmem_limit_bytes=20 * MIB),
        cost_estimate=pl.CostEstimate(
            flops=0, bytes_accessed=4 * 2 * pool * block * width, transcendentals=0
        ),
        name="updated_caches",
    )(far(lens), far(slot_req), far(slot_block), keys, values, after, *[far(array) for array in caches])


def merge_kernel(local, steps, part_ref, mean_ref, level_ref, weight_ref, out_ref):
    holders = part_ref.shape[0]
    width = weight_ref.shape[0]
    heads = width // HD
    per = heads * steps
    count = local * per
    values = [part_ref[g, pl.ds(0, count), :].astype(F32) for g in range(holders)]
    row = iota((count, HD), 0)
    lane = iota((count, HD), 1)
    mine = (lane % per == row % per) & (lane < 3 * per)
    levels = []
    for g in range(holders):
        stat = part_ref[g, pl.ds(count, 16), :].astype(F32)
        wide = jnp.concatenate(
            [jnp.broadcast_to(stat[j : j + 1], (per, HD)) for j in range(local)], axis=0
        )
        levels.append(jnp.sum(jnp.where(mine, wide, 0.0), axis=-1, keepdims=True))
    values.append(mean_ref[...])
    levels.append(level_ref[:, :1])
    top = functools.reduce(jnp.maximum, levels)
    shares = [jnp.exp(level - top) for level in levels]
    total = sum(shares)
    mixed = sum(share * value for share, value in zip(shares, values))
    attended = (mixed / total).astype(BF16)
    target = iota((GROUP, count), 0)
    source = iota((GROUP, count), 1)
    parts = []
    for h in range(heads):
        pick = (source == target // steps * per + h * steps + target % steps) & (
            target < local * steps
        )
        parts.append(dot_nn(pick.astype(BF16), attended).astype(BF16))
    out_ref[...] = dot_nn(jnp.concatenate(parts, axis=1), weight_ref[...]).astype(BF16)


def merge_project(parts, mean, level, out_weight, local, steps):
    return pl.pallas_call(
        functools.partial(merge_kernel, local, steps),
        out_shape=jax.ShapeDtypeStruct((GROUP, out_weight.shape[1]), BF16),
        in_specs=[vmem()] * 4,
        out_specs=vmem(),
        compiler_params=pltpu.CompilerParams(vmem_limit_bytes=8 * MIB),
        name="merge_project",
    )(parts, mean, level, out_weight)


def second_norm_kernel(hidden_ref, left_ref, right_ref, gain_ref, ids_ref, gates_ref, rows_out, res_out, rows_ref):
    local, steps, width = hidden_ref.shape
    rows_ref[...] = jnp.zeros_like(rows_ref)
    for j in range(local):
        rows_ref[pl.ds(j * steps, steps), :] = hidden_ref[j]
    residual = rows_ref[...] + (left_ref[...].astype(F32) + right_ref[...].astype(F32))
    res_out[...] = residual
    mean_square = jnp.mean(residual * residual, axis=-1, keepdims=True)
    normed = residual * lax.rsqrt(mean_square + 1e-06) * gain_ref[...]
    rows_out[:, pl.ds(0, width)] = normed.astype(BF16)
    rows_ref[:, pl.ds(0, HD)] = jnp.zeros((GROUP, HD), F32)
    lane = iota((steps, HD), 1)
    for j in range(local):
        table = jnp.zeros((steps, HD), F32)
        for k in range(ids_ref.shape[2]):
            hit = lane % EXPERTS == ids_ref[j, :, k : k + 1]
            table = table + jnp.where(hit, gates_ref[j, :, k : k + 1], 0.0)
        rows_ref[pl.ds(j * steps, steps), pl.ds(0, HD)] = table
    table = rows_ref[:, pl.ds(0, HD)]
    high = table.astype(BF16)
    low = (table - high.astype(F32)).astype(BF16)
    rows_out[:, pl.ds(width, HD)] = jnp.where(iota((GROUP, HD), 1) < EXPERTS, high.astype(F32), low.astype(F32)).astype(BF16)


def second_norm(hidden, left, right, gain, ids, gates):
    width = hidden.shape[2]
    return pl.pallas_call(
        second_norm_kernel,
        out_shape=(
            jax.ShapeDtypeStruct((GROUP, width + HD), BF16),
            jax.ShapeDtypeStruct((GROUP, width), F32),
        ),
        in_specs=[vmem()] * 6,
        out_specs=(vmem(), vmem()),
        scratch_shapes=[pltpu.VMEM((GROUP, width), F32)],
        compiler_params=pltpu.CompilerParams(vmem_limit_bytes=4 * MIB),
        name="second_norm",
    )(hidden, left, right, gain.reshape(1, width), ids, gates)


def shared_window(total, ranks):
    each = total // ranks
    length = max(-(-(r * each % 16 + each) // 16) * 16 for r in range(ranks))
    return each, length


def expert_blocks(hidden, every):
    blocks = [(low, min(low + BLOCK, every)) for low in range(0, every, BLOCK)]
    return blocks, min(FETCHED, sum(high <= hidden for _, high in blocks))


def fetch_kernel(low, rows, _, gate_hbm, up_hbm, gate_ref, up_ref, sem):
    copies = [
        pltpu.make_async_copy(source.at[pl.ds(low, rows)], target, sem.at[n])
        for n, (source, target) in enumerate(((gate_hbm, gate_ref), (up_hbm, up_ref)))
    ]
    for copy in copies:
        copy.start()
    for copy in copies:
        copy.wait()


def fetch(block, gate, up, after):
    low, high = block
    shape = pltpu.VMEM((high - low, gate.shape[1]), BF16)
    return pl.pallas_call(
        functools.partial(fetch_kernel, low, high - low),
        out_shape=(shape, shape),
        in_specs=[hbm()] * 3,
        out_specs=(vmem(), vmem()),
        scratch_shapes=[pltpu.SemaphoreType.DMA((2,))],
        compiler_params=pltpu.CompilerParams(vmem_limit_bytes=MIB),
        cost_estimate=pl.CostEstimate(
            flops=0, bytes_accessed=4 * (high - low) * gate.shape[1], transcendentals=0
        ),
        name="fetch_weights",
    )(after, far(gate), far(up))


def packs(tokens, columns):
    return tokens == 12 and columns == 4 * HD


def experts_kernel(
    tokens,
    count,
    ranks,
    fetched,
    rows_ref,
    *refs,
):
    early = [(refs[2 * i], refs[2 * i + 1]) for i in range(fetched)]
    streamed_experts(tokens, count, ranks, early, rows_ref, *refs[2 * fetched :])


def streamed_experts(
    tokens,
    count,
    ranks,
    early,
    rows_ref,
    gate_hbm,
    up_hbm,
    down_ref,
    shared_gate_hbm,
    shared_up_hbm,
    shared_down_hbm,
    out_ref,
    gate_ref,
    up_ref,
    shared_down_ref,
    inner_ref,
    total_ref,
    sem,
    shared_sem,
):
    hidden, width = gate_hbm.shape
    every = hidden + shared_down_ref.shape[0]
    each = hidden // count
    slim, length = shared_window(shared_gate_hbm.shape[0], ranks)
    seq_rank = lax.axis_index("seq")
    slim_low = seq_rank * slim
    slim_start = pl.multiple_of(
        jnp.minimum(slim_low // 16 * 16, shared_gate_hbm.shape[0] - length), 16
    )
    blocks, _ = expert_blocks(hidden, every)
    skipped = blocks[len(early) - 1][1] if early else 0

    def moves(source, extra, target, n, skip):
        copies = []
        for i, (low, high) in enumerate(blocks):
            top = min(high, hidden)
            piece = []
            if low < skip:
                continue
            if top > low:
                piece.append(
                    pltpu.make_async_copy(
                        source.at[pl.ds(low, top - low)],
                        target.at[pl.ds(low - skip, top - low)],
                        sem.at[n, i],
                    )
                )
            if high == every:
                piece.append(
                    pltpu.make_async_copy(
                        extra.at[pl.ds(slim_start, length)],
                        target.at[pl.ds(hidden - skip, length)],
                        shared_sem.at[n],
                    )
                )
            copies.append(piece)
        return copies

    gates = moves(gate_hbm, shared_gate_hbm, gate_ref, 0, skipped)
    ups = moves(up_hbm, shared_up_hbm, up_ref, 1, skipped)
    shared_down = pltpu.make_async_copy(
        shared_down_hbm.at[pl.ds(slim_start, length)], shared_down_ref, shared_sem.at[2]
    )
    stream = Stream([a + b for a, b in zip(gates, ups)] + [[shared_down]], 3)

    first = seq_rank * count
    rows = rows_ref[:, pl.ds(0, width)]
    table = rows_ref[:, pl.ds(width, HD)]
    for i, (low, high) in enumerate(blocks):
        shape = (HD, high - low)
        unit = low + iota(shape, 1)
        expert = jnp.where(unit < hidden, first + unit // each, -1)
        share = dot_nn(table, (iota(shape, 0) % EXPERTS == expert).astype(BF16))
        if high > hidden:
            unit = low + iota(share.shape, 1) - hidden + slim_start
            mine = (unit >= slim_low) & (unit < slim_low + slim)
            in_shared = low + iota(share.shape, 1) >= hidden
            share = jnp.where(in_shared, mine.astype(F32), share)
        if i < len(early):
            gate_block, up_block = (ref[...] for ref in early[i])
        else:
            stream.need(i + 1 - len(early))
            gate_block = gate_ref[pl.ds(low - skipped, high - low), :]
            up_block = up_ref[pl.ds(low - skipped, high - low), :]
        gate = dot_nt(rows, gate_block)
        up = dot_nt(rows, up_block)
        inner_ref[:, pl.ds(low, high - low)] = (jax.nn.silu(gate) * up * share).astype(BF16)

    groups = total_ref.shape[0] // GROUP
    pieces = out_ref.shape[0] // groups
    columns = width // pieces
    for i, (low, high) in enumerate(blocks):
        top = min(high, hidden)
        part = inner_ref[:, pl.ds(low, top - low)]
        if high == every:
            stream.need(len(gates) + 1)
            extra = inner_ref[:, pl.ds(hidden, length)]
        for p in range(pieces):
            cut = pl.ds(p * columns, columns)
            sums = dot_nn(part, down_ref[pl.ds(low, top - low), cut])
            if high == every:
                sums = sums + dot_nn(extra, shared_down_ref[:, cut])
            if i > 0:
                sums = sums + total_ref[:, cut]
            if i < len(blocks) - 1:
                total_ref[:, cut] = sums
            elif packs(tokens, columns):
                last = sums[:, 3 * HD :]
                body_row = iota(last.shape, 0) % GROUP < tokens
                for c in range(3):
                    moved = pltpu.roll(last, tokens - 4 * c, 0)
                    tile = jnp.where(body_row, sums[:, c * HD : (c + 1) * HD], moved).astype(BF16)
                    for g in range(groups):
                        out_ref[g * pieces + p, pl.ds(c * GROUP, GROUP), :] = tile[
                            g * GROUP : (g + 1) * GROUP
                        ]
            else:
                for g in range(groups):
                    out_ref[g * pieces + p] = sums[g * GROUP : g * GROUP + tokens].astype(BF16)


def all_experts(rows, early, routed, shared, tokens, pieces):
    count, each, width = routed[2].shape
    hidden = count * each
    groups = rows.shape[0] // GROUP
    every = hidden + shared_window(shared[2].shape[0], groups)[1]
    routed = [array.reshape(hidden, width) for array in routed]
    early = [array for pair in early for array in pair]
    shape = (tokens, width // pieces)
    if packs(*shape):
        shape = (3 * GROUP, HD)
    rest = every - sum(array.shape[0] for array in early) // 2
    return pl.pallas_call(
        functools.partial(experts_kernel, tokens, count, groups, len(early) // 2),
        out_shape=jax.ShapeDtypeStruct((groups * pieces, *shape), BF16),
        in_specs=[vmem()] * (1 + len(early)) + [hbm()] * 2 + [vmem()] + [hbm()] * 3,
        out_specs=vmem(),
        scratch_shapes=[pltpu.VMEM((rest, width), BF16)] * 2
        + [
            pltpu.VMEM((every - hidden, width), BF16),
            pltpu.VMEM((rows.shape[0], every), BF16),
            pltpu.VMEM((rows.shape[0], width), F32),
            pltpu.SemaphoreType.DMA((3, -(-every // BLOCK))),
            pltpu.SemaphoreType.DMA((3,)),
        ],
        compiler_params=pltpu.CompilerParams(
            vmem_limit_bytes=2 * rest * width * 2 + 8 * MIB
        ),
        name="experts",
    )(rows, *[near(array) for array in early], far(routed[0]), far(routed[1]), near(routed[2]), *[far(array) for array in shared])


def last_kernel(res_ref, parts_ref, out_ref):
    local, steps, columns = out_ref.shape
    total = parts_ref[0].astype(F32)
    for i in range(1, parts_ref.shape[0]):
        total = total + parts_ref[i].astype(F32)
    cut = pl.ds(pl.multiple_of(lax.axis_index("exp") * columns, HD), columns)
    for j in range(local):
        rows = slice(j * steps, (j + 1) * steps)
        own = res_ref[pl.ds(j * steps, steps), cut]
        if packs(local * steps, columns):
            for c in range(4):
                start = c * GROUP + j * steps if c < 3 else j * GROUP + local * steps
                lanes = slice(c * HD, (c + 1) * HD)
                out_ref[j, :, lanes] = own[:, lanes] + total[start : start + steps]
        else:
            out_ref[j] = own + total[rows]


def last_sum(residual, parts, local, steps, columns):
    return pl.pallas_call(
        last_kernel,
        out_shape=jax.ShapeDtypeStruct((local, steps, columns), F32),
        in_specs=[vmem(), vmem()],
        out_specs=vmem(),
        compiler_params=pltpu.CompilerParams(vmem_limit_bytes=8 * MIB),
        name="last_sum",
    )(residual, parts)


def partner(array, axis, bit):
    count = lax.axis_size(axis)
    return lax.ppermute(array, axis, [(i, i ^ bit) for i in range(count)])


def body(
    hidden_in,
    cache_lens,
    slot_request,
    slot_block,
    key_cache,
    value_cache,
    attn_gain,
    query_weight,
    key_weight,
    value_weight,
    out_weight,
    ffn_gain,
    expert_ids,
    expert_weights,
    gate_experts,
    up_experts,
    down_experts,
    gate_shared,
    up_shared,
    down_shared,
):
    local, steps, width = hidden_in.shape
    exp_count = lax.axis_size("exp")
    tokens = local * steps

    normed = norm_rows(hidden_in, attn_gain)
    rows = lax.all_gather(normed, "seq", axis=0, tiled=True)
    parts, queries = attention(
        rows,
        query_weight,
        (key_cache, value_cache),
        cache_lens,
        slot_request,
        slot_block,
        local,
        steps,
    )
    parts = lax.all_to_all(parts, "seq", split_axis=0, concat_axis=0, tiled=True)
    new_keys, new_values, mean, level = fresh_rows(
        rows, queries, (key_weight, value_weight), cache_lens, local, steps
    )
    terms = merge_project(parts, mean, level, out_weight, local, steps)
    gate_rows = jnp.swapaxes(gate_experts, 1, 2).reshape(-1, width)
    up_rows = jnp.swapaxes(up_experts, 1, 2).reshape(-1, width)
    hidden = gate_rows.shape[0]
    extra = shared_window(down_shared.shape[0], lax.axis_size("seq"))[1]
    blocks, fetched = expert_blocks(hidden, hidden + extra)
    early = []
    other = partner(terms, "exp", 1)
    bit = 2
    while bit < exp_count:
        if len(early) < fetched:
            early.append(fetch(blocks[len(early)], gate_rows, up_rows, terms))
            other, early[-1] = lax.optimization_barrier((other, early[-1]))
        terms = (terms.astype(F32) + other.astype(F32)).astype(BF16)
        other = partner(terms, "exp", bit)
        bit *= 2
    while len(early) < fetched:
        early.append(fetch(blocks[len(early)], gate_rows, up_rows, terms))
    ffn_in, residual = second_norm(
        hidden_in, terms, other, ffn_gain, expert_ids, expert_weights
    )
    all_rows = lax.all_gather(ffn_in, "seq", axis=0, tiled=True)
    sums = all_experts(
        all_rows,
        early,
        (jnp.swapaxes(gate_experts, 1, 2), jnp.swapaxes(up_experts, 1, 2), down_experts),
        (jnp.swapaxes(gate_shared, 0, 1), jnp.swapaxes(up_shared, 0, 1), down_shared),
        tokens,
        exp_count,
    )
    key_out, value_out = updated_caches(
        (key_cache, value_cache),
        new_keys,
        new_values,
        cache_lens,
        slot_request,
        slot_block,
        sums,
        local,
        steps,
    )
    sums = lax.all_to_all(sums, ("seq", "exp"), split_axis=0, concat_axis=0, tiled=True)
    hidden_out = last_sum(residual, sums, local, steps, width // exp_count)
    return hidden_out, key_out, value_out


def solution(mesh):
    in_specs = (
        P("seq", None, None),
        P(),
        P("seq"),
        P("seq"),
        P("seq", None, "exp"),
        P("seq", None, "exp"),
        P(),
        P(None, "exp"),
        P(None, "exp"),
        P(None, "exp"),
        P("exp", None),
        P(),
        P("seq", None, None),
        P("seq", None, None),
        P("seq", None, "exp"),
        P("seq", None, "exp"),
        P("seq", "exp", None),
        P(None, "exp"),
        P(None, "exp"),
        P("exp", None),
    )
    out_specs = (P("seq", None, "exp"), P("seq", None, "exp"), P("seq", None, "exp"))
    return jax.shard_map(body, mesh=mesh, in_specs=in_specs, out_specs=out_specs, check_vma=False)
```
